256 devices in a mesh: fsdp: 16 (over y, x), rep: 16 (over z, core).
Axes of the slice: x: 4, y: 4, z: 8, core: 2. Of those that a mesh axis runs over, the one named last changes fastest.
Arguments:
- grad_parts: bfloat16 [16, 8192, 4096], P('rep', 'fsdp'), may hold values from -170 to 170
- owner_table: int32 [32], replicated, may hold values from 0 to 31, each once
- left_stats: float32 [512, 256, 256], P(('fsdp', 'rep')), may hold values from -1e-05 to 1e-05, as said below
- right_stats: float32 [512, 256, 256], P(('fsdp', 'rep')), may hold values from -1e-05 to 1e-05, as said below
- accum: float32 [512, 256, 256], P(('fsdp', 'rep')), may hold values from 1e-08 to 1e-06
- master: float32 [512, 256, 256], P(('fsdp', 'rep')), may hold values from -1.5 to 1.5
Outputs:
- steps: float32 [512, 256, 256], P(('fsdp', 'rep'))
- weights_new: bfloat16 [8192, 4096], P('fsdp')
The draws below stay inside these ranges and needn't reach their ends.
Inputs may be any that keep to these rules, and one draw needn't show every extreme that they name: owner_table is a permutation of the 32 local tile ids; the device at index r of rep owns the slots r * 2 to (r + 1) * 2 - 1 of its row band. `left_stats`: each slot's matrix is symmetric positive definite. `right_stats`: each slot's matrix is symmetric positive definite.
All inputs are finite; a program needn't handle non-finite values.
Results may differ from the reference program's by a relative error of at most 0.001.
Values may be sent and summed in bfloat16 or wider, within the bound.
A program may use at most 64 MiB of HBM per device.

```python
import math
import jax
import jax.numpy as jnp
from jax import lax

D = 8192
F = 4096
BLK = 256
ITERS = 8
RB = 2
CB = 16
NBS = 32
NBLK = 512
N_FSDP = 16
N_REP = 16


def draw_grad_parts(key, part):
    key = jax.random.fold_in(key, 11)
    first = jax.random.fold_in(key, 0)
    second = jax.random.fold_in(key, 1)
    third = jax.random.fold_in(key, 2)
    fifth = jax.random.fold_in(key, 4)
    sixth = jax.random.fold_in(key, 5)
    rising = 3.0 ** (jnp.arange(D, dtype=jnp.float32) / (D - 1))
    row_scale = jnp.exp(jax.random.uniform(first, (D,), dtype=jnp.float32) * math.log(10.0)) * rising
    col_scale = jnp.exp(jax.random.uniform(second, (F,), dtype=jnp.float32) * math.log(10.0))
    half_span = 0.5 * math.log(10.0)
    band_factor = jnp.exp(jax.random.uniform(fifth, (N_REP, N_FSDP), dtype=jnp.float32, minval=-half_span, maxval=half_span))
    column_factor = jnp.exp(jax.random.uniform(sixth, (N_REP, F // BLK), dtype=jnp.float32, minval=-half_span, maxval=half_span))
    band_rows = jnp.repeat(band_factor, D // N_FSDP, axis=1)
    column_cols = jnp.repeat(column_factor, BLK, axis=1)
    noise = jnp.clip(jax.random.normal(third, (N_REP, D, F), dtype=jnp.float32), -6.0, 6.0)
    values = 0.05 * noise * row_scale[None, :, None] * col_scale[None, None, :]
    values = values * band_rows[:, :, None] * column_cols[:, None, :]
    values = jnp.clip(values, -170.0, 170.0)
    return values.astype(jnp.bfloat16)


def spd_stats(key, strength):
    first, second = jax.random.split(key)
    logs = jax.random.uniform(first, (NBLK, BLK), dtype=jnp.float32, minval=math.log(1e-07), maxval=math.log(1e-05))
    diag = jnp.exp(logs)
    raw = jax.random.uniform(second, (NBLK, BLK, BLK), dtype=jnp.float32, minval=-1.0, maxval=1.0)
    sym = 0.5 * (raw + jnp.swapaxes(raw, 1, 2))
    identity = jnp.eye(BLK, dtype=jnp.float32)
    mixed = identity + strength / BLK * sym * (1.0 - identity)
    root_diag = jnp.sqrt(diag)
    return root_diag[:, :, None] * mixed * root_diag[:, None, :]


def draw_left_stats(key, part):
    key = jax.random.fold_in(key, 21)
    return spd_stats(key, 0.5)


def draw_right_stats(key, part):
    key = jax.random.fold_in(key, 31)
    return spd_stats(key, 0.5)


def shard_levels(key, dims, cuts, low, top_value):
    def one(axis_at, shards_of):
        draws = jax.random.uniform(jax.random.fold_in(jax.random.fold_in(key, 6), axis_at), (shards_of,), jnp.float32, low / len(cuts), top_value / len(cuts))
        return jnp.repeat(jnp.exp(draws), dims[axis_at] // shards_of).reshape((-1,) + (1,) * (len(dims) - axis_at - 1))

    factor_of = one(*cuts[0])
    for cut in cuts[1:]:
        factor_of = factor_of * one(*cut)
    return factor_of


def gaussian(stream_key, extent, scale, most, cuts=(), kind=jnp.bfloat16):
    entries = scale * jax.random.normal(stream_key, extent, jnp.float32)
    if cuts:
        entries = entries * shard_levels(stream_key, extent, cuts, -0.22, 0.18)
    return jnp.clip(entries, -most, most).astype(kind)


def setup_inputs(seed: int = 0) -> dict:
    key_of = jax.random.split(jax.random.key(seed), 7)
    grad_parts = draw_grad_parts(jax.random.fold_in(key_of[6], 71), 0)
    owner_table = jax.random.permutation(key_of[1], NBS).astype(jnp.int32)
    left_stats = draw_left_stats(jax.random.fold_in(key_of[6], 71), 0)
    right_stats = draw_right_stats(jax.random.fold_in(key_of[6], 71), 0)
    accum = jnp.clip(jnp.exp(math.log(9.999999974752427e-07) - 4.6051702 * jax.random.uniform(key_of[4], (NBLK, BLK, BLK), jnp.float32) ** shard_levels(key_of[4], (NBLK, BLK, BLK), ((0, 256),), -0.2, 0.2)), 9.99999993922529e-09, 9.999999974752427e-07)
    master = gaussian(key_of[5], (NBLK, BLK, BLK), 0.25, 1.5, ((0, 256),), jnp.float32)
    return dict(grad_parts=grad_parts, owner_table=owner_table, left_stats=left_stats, right_stats=right_stats, accum=accum, master=master)


EPSILON = 1e-06
STEP_RATE = 0.2
CLIP_NORM = 1.0

def product(left, right):
    return jnp.einsum('bij,bjk->bik', left, right, precision=lax.Precision.HIGHEST)

def inverse_root(matrix):
    width = matrix.shape[-1]
    identity = jnp.eye(width, dtype=jnp.float32)
    regular = matrix + EPSILON * identity
    frobenius = jnp.sqrt(lax.optimization_barrier(jnp.sum(regular * regular, axis=(1, 2), keepdims=True)))
    zeta = 2.5 / frobenius
    current = zeta * regular
    root_est = zeta ** 0.25 * identity
    for sweep in range(ITERS):
        factor = (5.0 * identity - current) / 4.0
        root_est = product(root_est, factor)
        square = product(factor, factor)
        current = product(product(square, square), current)
    return root_est

def precondition(scaled, left_new, right_new, accum):
    left_root = inverse_root(left_new)
    right_root = inverse_root(right_new)
    shampoo = product(product(left_root, scaled), right_root)
    adagrad = scaled / (jnp.sqrt(accum + scaled * scaled) + EPSILON)
    ada_size = jnp.sqrt(lax.optimization_barrier(jnp.sum(adagrad * adagrad, axis=(1, 2), keepdims=True)))
    sham_size = jnp.sqrt(lax.optimization_barrier(jnp.sum(shampoo * shampoo, axis=(1, 2), keepdims=True)))
    return shampoo * (ada_size / (sham_size + EPSILON))

def shard_step(inputs):
    scaled, left, right, acc_part = inputs
    left_new = left + jnp.einsum('bij,bkj->bik', scaled, scaled, precision=lax.Precision.HIGHEST)
    right_new = right + jnp.einsum('bji,bjk->bik', scaled, scaled, precision=lax.Precision.HIGHEST)
    return precondition(scaled, left_new, right_new, acc_part)

def by_band(array):
    return array.reshape(N_FSDP, NBS, BLK, BLK)

def reference(grad_parts, owner_table, left_stats, right_stats, accum, master):
    total_grad = lax.optimization_barrier(jnp.sum(grad_parts, axis=0, dtype=jnp.float32))
    clip = jnp.minimum(1.0, CLIP_NORM / (jnp.sqrt(jnp.sum(total_grad * total_grad)) + EPSILON))
    scaled_full = clip * total_grad
    tiles = scaled_full.reshape(N_FSDP, RB, BLK, CB, BLK).transpose(0, 1, 3, 2, 4).reshape(N_FSDP, NBS, BLK, BLK)
    slotted = jnp.take(tiles, owner_table, axis=1)
    steps = lax.map(shard_step, (slotted, by_band(left_stats), by_band(right_stats), by_band(accum)))
    fresh = (by_band(master) - STEP_RATE * steps).astype(jnp.bfloat16)
    inverse = jnp.argsort(owner_table).astype(jnp.int32)
    placed = jnp.take(fresh, inverse, axis=1)
    weights_new = placed.reshape(N_FSDP, RB, CB, BLK, BLK).transpose(0, 1, 3, 2, 4).reshape(D, F)
    return (steps.reshape(NBLK, BLK, BLK), weights_new)
```

```python
import functools
import jax
import jax.numpy as jnp
from jax import lax
from jax.experimental import pallas as pl
from jax.experimental.pallas import tpu as pltpu
from jax.sharding import PartitionSpec as P

ITERS = 8
EPSILON = 1e-06
STEP_RATE = 0.2
CLIP_NORM = 1.0
W = 256
LEVELS = 32767.0
TINY = 1e-30
f32, bf16, i16 = jnp.float32, jnp.bfloat16, jnp.int16
MESH = pl.DeviceIdType.MESH

OFFSETS = (4, -3, 3, -2, 2, -1, 1, 0)
RS_HOPS = (4, 3, 3, 2, 2, 1, 1)
AG_HOPS = (1, 1, 2, 2, 3, 3, 4)
PICK = ((0, 1, 0, 1, 0, 1, 0), (1, 0, 1, 0, 1, 0, 1))
SIGN = (-1, 1)


def split(x):
    high = x.astype(bf16)
    return high, (x - high.astype(f32)).astype(bf16)


def dot(a, b):
    return jnp.dot(a, b, preferred_element_type=f32)


def mm(a, b):
    return dot(a[0], b[0]) + (dot(a[0], b[1]) + dot(a[1], b[0]))


def gram_left(a):
    def one(u, v):
        return lax.dot_general(u, v, (((1,), (1,)), ((), ())), preferred_element_type=f32)

    return one(a[0], a[0]) + (one(a[0], a[1]) + one(a[1], a[0]))


def gram_right(a):
    def one(u, v):
        return lax.dot_general(u, v, (((0,), (0,)), ((), ())), preferred_element_type=f32)

    return one(a[0], a[0]) + (one(a[0], a[1]) + one(a[1], a[0]))


def eye():
    rows = lax.broadcasted_iota(jnp.int32, (W, W), 0)
    return (rows == lax.broadcasted_iota(jnp.int32, (W, W), 1)).astype(f32)


def spread(scale):
    tall = jnp.concatenate([scale] * 4, axis=0)
    return jnp.concatenate([tall, tall], axis=1)


def fold(x, op):
    parts = [x[8 * i : 8 * i + 8, :] for i in range(4)]
    both = op(op(parts[0], parts[1]), op(parts[2], parts[3]))
    return op(both[:, :128], both[:, 128:])


def kernel(
    table, band_h, left_h, right_h, accum_h, master_h,
    steps, gath,
    band, left, right, accum, master,
    stage, sib, total, sendq, sends, recvq, recvs, summed, ag, nsend, nrecv,
    mats, roots,
    in_sem, sib_ssem, sib_rsem, q_ssem, q_rsem, s_ssem, s_rsem,
    n_ssem, n_rsem, ag_ssem, ag_rsem, x_ssem, x_rsem, out_sem,
):
    f = lax.axis_index("fsdp")
    r = lax.axis_index("rep")
    z = r // 2
    c = r - 2 * z
    mate = {"rep": r + 1 - 2 * c}
    chips = 8

    def near(step):
        return {"rep": 2 * lax.rem(z + step + chips, chips) + c}

    def at(step):
        return lax.rem(z + step + chips, chips)

    barrier = pltpu.get_barrier_semaphore()
    for o in range(1, 16):
        pl.semaphore_signal(barrier, 1, device_id={"rep": lax.rem(r + o, 16)}, device_id_type=MESH)
        pl.semaphore_signal(barrier, 1, device_id={"fsdp": lax.rem(f + o, 16)}, device_id_type=MESH)

    loads = [
        pltpu.make_async_copy(
            band_h.at[pl.ds(W * (t // 16), W), pl.ds(W * (t % 16), W)], band.at[t], in_sem.at[0]
        )
        for t in range(32)
    ] + [
        pltpu.make_async_copy(left_h, left, in_sem.at[1]),
        pltpu.make_async_copy(right_h, right, in_sem.at[2]),
        pltpu.make_async_copy(accum_h, accum, in_sem.at[3]),
        pltpu.make_async_copy(master_h, master, in_sem.at[4]),
    ]
    for load in loads:
        load.start()
    pltpu.make_async_copy(band, band, in_sem.at[0]).wait()

    def to_mate(j):
        return pltpu.make_async_remote_copy(
            src_ref=stage.at[j], dst_ref=sib.at[j], send_sem=sib_ssem.at[j], recv_sem=sib_rsem.at[j],
            device_id=mate, device_id_type=MESH,
        )

    def fill(j):
        for k in range(2):
            ident = table[4 * at(OFFSETS[j]) + 2 * (1 - c) + k]
            stage[j, pl.ds(k * W, W), :] = band[ident]

    for j in range(8):
        fill(j)
        if j == 0:
            pl.semaphore_wait(barrier, 30)
        to_mate(j).start()

    def pair(j, k, i, ident):
        own = band[ident, pl.ds(32 * i, 32), :].astype(f32)
        return own + sib[j, pl.ds(k * W + 32 * i, 32), :].astype(f32)

    def arrived(d, m, i):
        return recvq[d, m, pl.ds(32 * i, 32), :].astype(f32) * spread(recvs[d, m])

    def data_copy(d, m):
        return pltpu.make_async_remote_copy(
            src_ref=sendq.at[d, m], dst_ref=recvq.at[d, m], send_sem=q_ssem.at[d, m], recv_sem=q_rsem.at[d, m],
            device_id=near(SIGN[d]), device_id_type=MESH,
        )

    def scale_copy(d, m):
        return pltpu.make_async_remote_copy(
            src_ref=sends.at[d, m], dst_ref=recvs.at[d, m], send_sem=s_ssem.at[d, m], recv_sem=s_rsem.at[d, m],
            device_id=near(SIGN[d]), device_id_type=MESH,
        )

    def message(d, m):
        j = OFFSETS.index(SIGN[d] * RS_HOPS[m]) if RS_HOPS[m] != 4 else 0
        k = PICK[d][m]
        ident = table[4 * at(OFFSETS[j]) + 2 * c + k]
        if m >= 2:
            data_copy(d, m - 2).wait_recv()
            scale_copy(d, m - 2).wait_recv()
        most = jnp.full((8, 128), TINY, f32)
        for i in range(8):
            x = pair(j, k, i, ident)
            if m >= 2:
                x = x + arrived(d, m - 2, i)
            total[d, pl.ds(32 * i, 32), :] = x
            most = jnp.maximum(most, fold(jnp.abs(x), jnp.maximum))
        sends[d, m] = most * (1.0 / LEVELS)
        inverse = spread(LEVELS / most)
        for i in range(8):
            x = total[d, pl.ds(32 * i, 32), :] * inverse
            sendq[d, m, pl.ds(32 * i, 32), :] = jnp.round(x).astype(jnp.int32).astype(i16)
        data_copy(d, m).start()
        scale_copy(d, m).start()

    waited = set()
    for m in range(7):
        for d in range(2):
            j = OFFSETS.index(SIGN[d] * RS_HOPS[m]) if RS_HOPS[m] != 4 else 0
            if j not in waited:
                to_mate(j).wait_recv()
                waited.add(j)
            message(d, m)
    to_mate(7).wait_recv()
    for d in range(2):
        for m in (5, 6):
            data_copy(d, m).wait_recv()
            scale_copy(d, m).wait_recv()
    size = jnp.zeros((8, 128), f32)
    for k in range(2):
        ident = table[4 * z + 2 * c + k]
        for i in range(8):
            x = pair(7, k, i, ident)
            for d in range(2):
                m = 5 if PICK[d][5] == k else 6
                x = x + arrived(d, m, i)
            summed[k, pl.ds(32 * i, 32), :] = x
            size = size + fold(x * x, jnp.add)

    def norm_copy(stg, o):
        peer = {"rep": lax.rem(r + o, 16)} if stg == 0 else {"fsdp": lax.rem(f + o, 16)}
        return pltpu.make_async_remote_copy(
            src_ref=nsend.at[stg], dst_ref=nrecv.at[stg, o - 1], send_sem=n_ssem.at[stg], recv_sem=n_rsem.at[stg],
            device_id=peer, device_id_type=MESH,
        )

    def norm_all(stg):
        return pltpu.make_async_copy(nrecv.at[stg], nrecv.at[stg], n_rsem.at[stg])

    nsend[0] = size
    for o in range(1, 16):
        norm_copy(0, o).start()

    for load in loads[32:]:
        load.wait()
    for k in range(2):
        parts = split(summed[k])
        mats[2 * k] = gram_left(parts)
        mats[2 * k + 1] = gram_right(parts)

    norm_all(0).wait()
    for o in range(15):
        size = size + nrecv[0, o]
    nsend[1] = size
    for o in range(1, 16):
        norm_copy(1, o).start()
    norm_all(1).wait()
    for o in range(15):
        size = size + nrecv[1, o]
    norm_sq = jnp.sum(size, keepdims=True)
    clip = jnp.minimum(1.0, CLIP_NORM / (jnp.sqrt(norm_sq) + EPSILON))

    ident = eye()
    for k in range(2):
        for s in range(2):
            stats = left if s == 0 else right
            t = 2 * k + s
            a = stats[k] + (clip * clip) * mats[t] + EPSILON * ident
            zeta = 2.5 / jnp.sqrt(jnp.sum(a * a, keepdims=True))
            cur = zeta * a
            p = 1.25 * ident - 0.25 * cur
            roots[t] = jnp.sqrt(jnp.sqrt(zeta)) * p
            ps = split(p)
            ss = split(mm(ps, ps))
            qs = split(mm(ss, ss))
            mats[t] = mm(qs, split(cur))

    def sweep(i, carry):
        curs = [mats[t] for t in range(4)]
        pss = [split(1.25 * ident - 0.25 * cur) for cur in curs]
        for t in range(4):
            roots[t] = mm(split(roots[t]), pss[t])
        sss = [split(mm(p, p)) for p in pss]
        qss = [split(mm(s, s)) for s in sss]
        for t in range(4):
            mats[t] = mm(qss[t], split(curs[t]))
        return carry

    lax.fori_loop(0, ITERS - 2, sweep, 0)
    for t in range(4):
        p = 1.25 * ident - 0.25 * mats[t]
        roots[t] = mm(split(roots[t]), split(p))

    for k in range(2):
        g = clip * summed[k]
        sham = mm(split(mm(split(roots[2 * k]), split(g))), split(roots[2 * k + 1]))
        ada = g / (jnp.sqrt(accum[k] + g * g) + EPSILON)
        ada_size = jnp.sqrt(jnp.sum(ada * ada, keepdims=True))
        sham_size = jnp.sqrt(jnp.sum(sham * sham, keepdims=True))
        step = sham * (ada_size / (sham_size + EPSILON))
        steps[k] = step
        ag[4 * z + 2 * c + k] = (master[k] - STEP_RATE * step).astype(bf16)

    def slot_of(d, m, back):
        origin = at(-SIGN[d] * (AG_HOPS[m] - back))
        return 4 * origin + 2 * c + PICK[d][m]

    def ag_copy(d, m):
        slot = slot_of(d, m, 1)
        return pltpu.make_async_remote_copy(
            src_ref=ag.at[slot], dst_ref=ag.at[slot], send_sem=ag_ssem.at[d, m], recv_sem=ag_rsem.at[d, m],
            device_id=near(SIGN[d]), device_id_type=MESH,
        )

    def ag_recv(d, m):
        slot = slot_of(d, m, 0)
        return pltpu.make_async_remote_copy(
            src_ref=ag.at[slot], dst_ref=ag.at[slot], send_sem=ag_ssem.at[d, m], recv_sem=ag_rsem.at[d, m],
            device_id=near(SIGN[d]), device_id_type=MESH,
        )

    def mate_copy(n, slot):
        return pltpu.make_async_remote_copy(
            src_ref=ag.at[slot], dst_ref=gath.at[slot], send_sem=x_ssem.at[n], recv_sem=x_rsem.at[n],
            device_id=mate, device_id_type=MESH,
        )

    def out_copy(n, slot):
        return pltpu.make_async_copy(ag.at[slot], gath.at[slot], out_sem.at[n])

    for m in range(2):
        for d in range(2):
            ag_copy(d, m).start()
    moves = []
    for k in range(2):
        moves.append((k, 4 * z + 2 * c + k))
        mate_copy(*moves[-1]).start()
        out_copy(*moves[-1]).start()
    for m in range(7):
        for d in range(2):
            ag_recv(d, m).wait_recv()
            if m + 2 < 7:
                ag_copy(d, m + 2).start()
            moves.append((2 + 2 * m + d, slot_of(d, m, 0)))
            mate_copy(*moves[-1]).start()
            out_copy(*moves[-1]).start()

    for move in moves:
        out_copy(*move).wait()
        mate_copy(*move).wait_send()
        mate_copy(*move).wait_recv()
    for d in range(2):
        for m in range(7):
            ag_copy(d, m).wait_send()
            data_copy(d, m).wait_send()
            scale_copy(d, m).wait_send()
    for j in range(8):
        to_mate(j).wait_send()
    for stg in range(2):
        norm_all_sent = pltpu.make_async_copy(nrecv.at[stg], nrecv.at[stg], n_ssem.at[stg])
        norm_all_sent.wait()


def place(table, gath, steps_in, weights, steps, sems):
    copies = [pltpu.make_async_copy(steps_in, steps, sems.at[32])]
    for s in range(32):
        ident = table[s]
        top = pl.multiple_of((ident // 16) * W, W)
        lead = pl.multiple_of((ident % 16) * W, W)
        copies.append(
            pltpu.make_async_copy(gath.at[s], weights.at[pl.ds(top, W), pl.ds(lead, W)], sems.at[s])
        )
    for copy in copies:
        copy.start()
    for copy in copies:
        copy.wait()


def per_device(grad_parts, owner_table, left_stats, right_stats, accum, master):
    band = grad_parts[0]
    smem = pl.BlockSpec(memory_space=pltpu.SMEM)
    anyw = pl.BlockSpec(memory_space=pl.ANY)
    vmem = pl.BlockSpec(memory_space=pltpu.VMEM)
    tiles = (2, W, W)
    dma = pltpu.SemaphoreType.DMA
    steps, gath = pl.pallas_call(
        kernel,
        out_shape=(
            jax.ShapeDtypeStruct(tiles, f32),
            jax.ShapeDtypeStruct((32, W, W), bf16),
        ),
        in_specs=[smem] + [anyw] * 5,
        out_specs=(vmem, anyw),
        scratch_shapes=[
            pltpu.VMEM((32, W, W), bf16),
            pltpu.VMEM(tiles, f32),
            pltpu.VMEM(tiles, f32),
            pltpu.VMEM(tiles, f32),
            pltpu.VMEM(tiles, f32),
            pltpu.VMEM((8, 2 * W, W), bf16),
            pltpu.VMEM((8, 2 * W, W), bf16),
            pltpu.VMEM(tiles, f32),
            pltpu.VMEM((2, 7, W, W), i16),
            pltpu.VMEM((2, 7, 8, 128), f32),
            pltpu.VMEM((2, 7, W, W), i16),
            pltpu.VMEM((2, 7, 8, 128), f32),
            pltpu.VMEM(tiles, f32),
            pltpu.VMEM((32, W, W), bf16),
            pltpu.VMEM((2, 8, 128), f32),
            pltpu.VMEM((2, 15, 8, 128), f32),
            pltpu.VMEM((4, W, W), f32),
            pltpu.VMEM((4, W, W), f32),
            dma((5,)), dma((8,)), dma((8,)), dma((2, 7)), dma((2, 7)), dma((2, 7)), dma((2, 7)),
            dma((2,)), dma((2,)), dma((2, 7)), dma((2, 7)), dma((16,)), dma((16,)), dma((16,)),
        ],
        compiler_params=pltpu.CompilerParams(
            collective_id=0, has_side_effects=True, vmem_limit_bytes=56 << 20
        ),
        name="shampoo",
    )(owner_table, band, left_stats, right_stats, accum, master)
    weights, steps = pl.pallas_call(
        place,
        out_shape=(
            jax.ShapeDtypeStruct(band.shape, bf16),
            jax.ShapeDtypeStruct(tiles, f32),
        ),
        in_specs=[smem, anyw, anyw],
        out_specs=(anyw, anyw),
        scratch_shapes=[dma((33,))],
        compiler_params=pltpu.CompilerParams(vmem_limit_bytes=56 << 20),
        name="place",
    )(owner_table, gath, steps)
    return (steps, weights)


def solution(mesh):
    return jax.shard_map(
        per_device,
        mesh=mesh,
        in_specs=(
            P("rep", "fsdp", None),
            P(),
            P(("fsdp", "rep"), None, None),
            P(("fsdp", "rep"), None, None),
            P(("fsdp", "rep"), None, None),
            P(("fsdp", "rep"), None, None),
        ),
        out_specs=(P(("fsdp", "rep"), None, None), P("fsdp", None)),
        check_vma=False,
    )
```

```python
import functools
import jax
import jax.numpy as jnp
from jax import lax
from jax.experimental import pallas as pl
from jax.experimental.pallas import tpu as pltpu
from jax.sharding import PartitionSpec as P

ITERS = 8
EPSILON = 1e-06
STEP_RATE = 0.2
CLIP_NORM = 1.0
W = 256
LEVELS = 32767.0
TINY = 1e-30
f32, bf16, i16 = jnp.float32, jnp.bfloat16, jnp.int16
MESH = pl.DeviceIdType.MESH

OFFSETS = (4, -3, 3, -2, 2, -1, 1, 0)
RS_HOPS = (4, 3, 3, 2, 2, 1, 1)
AG_HOPS = (1, 1, 2, 2, 3, 3, 4)
PICK = ((0, 1, 0, 1, 0, 1, 0), (1, 0, 1, 0, 1, 0, 1))
SIGN = (-1, 1)


def split(x):
    high = x.astype(bf16)
    return high, (x - high.astype(f32)).astype(bf16)


def dot(a, b):
    return jnp.dot(a, b, preferred_element_type=f32)


def mm(a, b):
    return dot(a[0], b[0]) + (dot(a[0], b[1]) + dot(a[1], b[0]))


def gram_left(a):
    def one(u, v):
        return lax.dot_general(u, v, (((1,), (1,)), ((), ())), preferred_element_type=f32)

    return one(a[0], a[0]) + (one(a[0], a[1]) + one(a[1], a[0]))


def gram_right(a):
    def one(u, v):
        return lax.dot_general(u, v, (((0,), (0,)), ((), ())), preferred_element_type=f32)

    return one(a[0], a[0]) + (one(a[0], a[1]) + one(a[1], a[0]))


def eye():
    rows = lax.broadcasted_iota(jnp.int32, (W, W), 0)
    return (rows == lax.broadcasted_iota(jnp.int32, (W, W), 1)).astype(f32)


def spread(scale):
    tall = jnp.concatenate([scale] * 4, axis=0)
    return jnp.concatenate([tall, tall], axis=1)


def fold(x, op):
    parts = [x[8 * i : 8 * i + 8, :] for i in range(4)]
    both = op(op(parts[0], parts[1]), op(parts[2], parts[3]))
    return op(both[:, :128], both[:, 128:])


def kernel(
    table, band_h, left_h, right_h, accum_h, master_h,
    steps, ag,
    band, left, right, accum, master,
    stage, sib, total, sendq, sends, recvq, recvs, summed, nsend, nrecv,
    mats, roots,
    in_sem, sib_ssem, sib_rsem, q_ssem, q_rsem, s_ssem, s_rsem,
    n_ssem, n_rsem, ag_ssem, ag_rsem, x_ssem, x_rsem,
):
    f = lax.axis_index("fsdp")
    r = lax.axis_index("rep")
    z = r // 2
    c = r - 2 * z
    mate = {"rep": r + 1 - 2 * c}
    chips = 8

    def near(step):
        return {"rep": 2 * lax.rem(z + step + chips, chips) + c}

    def at(step):
        return lax.rem(z + step + chips, chips)

    barrier = pltpu.get_barrier_semaphore()
    for o in range(1, 16):
        pl.semaphore_signal(barrier, 1, device_id={"rep": lax.rem(r + o, 16)}, device_id_type=MESH)
        pl.semaphore_signal(barrier, 1, device_id={"fsdp": lax.rem(f + o, 16)}, device_id_type=MESH)

    loads = [
        pltpu.make_async_copy(
            band_h.at[pl.ds(W * (t // 16), W), pl.ds(W * (t % 16), W)], band.at[t], in_sem.at[0]
        )
        for t in range(32)
    ] + [
        pltpu.make_async_copy(left_h, left, in_sem.at[1]),
        pltpu.make_async_copy(right_h, right, in_sem.at[2]),
        pltpu.make_async_copy(accum_h, accum, in_sem.at[3]),
        pltpu.make_async_copy(master_h, master, in_sem.at[4]),
    ]
    for load in loads:
        load.start()
    pltpu.make_async_copy(band, band, in_sem.at[0]).wait()

    def to_mate(j):
        return pltpu.make_async_remote_copy(
            src_ref=stage.at[j], dst_ref=sib.at[j], send_sem=sib_ssem.at[j], recv_sem=sib_rsem.at[j],
            device_id=mate, device_id_type=MESH,
        )

    def fill(j):
        for k in range(2):
            ident = table[4 * at(OFFSETS[j]) + 2 * (1 - c) + k]
            stage[j, pl.ds(k * W, W), :] = band[ident]

    for j in range(8):
        fill(j)
        if j == 0:
            pl.semaphore_wait(barrier, 30)
        to_mate(j).start()

    def pair(j, k, i, ident):
        own = band[ident, pl.ds(32 * i, 32), :].astype(f32)
        return own + sib[j, pl.ds(k * W + 32 * i, 32), :].astype(f32)

    def arrived(d, m, i):
        return recvq[d, m, pl.ds(32 * i, 32), :].astype(f32) * spread(recvs[d, m])

    def data_copy(d, m):
        return pltpu.make_async_remote_copy(
            src_ref=sendq.at[d, m], dst_ref=recvq.at[d, m], send_sem=q_ssem.at[d, m], recv_sem=q_rsem.at[d, m],
            device_id=near(SIGN[d]), device_id_type=MESH,
        )

    def scale_copy(d, m):
        return pltpu.make_async_remote_copy(
            src_ref=sends.at[d, m], dst_ref=recvs.at[d, m], send_sem=s_ssem.at[d, m], recv_sem=s_rsem.at[d, m],
            device_id=near(SIGN[d]), device_id_type=MESH,
        )

    def message(d, m):
        j = OFFSETS.index(SIGN[d] * RS_HOPS[m]) if RS_HOPS[m] != 4 else 0
        k = PICK[d][m]
        ident = table[4 * at(OFFSETS[j]) + 2 * c + k]
        if m >= 2:
            data_copy(d, m - 2).wait_recv()
            scale_copy(d, m - 2).wait_recv()
        most = jnp.full((8, 128), TINY, f32)
        for i in range(8):
            x = pair(j, k, i, ident)
            if m >= 2:
                x = x + arrived(d, m - 2, i)
            total[d, pl.ds(32 * i, 32), :] = x
            most = jnp.maximum(most, fold(jnp.abs(x), jnp.maximum))
        sends[d, m] = most * (1.0 / LEVELS)
        inverse = spread(LEVELS / most)
        for i in range(8):
            x = total[d, pl.ds(32 * i, 32), :] * inverse
            sendq[d, m, pl.ds(32 * i, 32), :] = jnp.round(x).astype(jnp.int32).astype(i16)
        data_copy(d, m).start()
        scale_copy(d, m).start()

    waited = set()
    for m in range(7):
        for d in range(2):
            j = OFFSETS.index(SIGN[d] * RS_HOPS[m]) if RS_HOPS[m] != 4 else 0
            if j not in waited:
                to_mate(j).wait_recv()
                waited.add(j)
            message(d, m)
    to_mate(7).wait_recv()
    for d in range(2):
        for m in (5, 6):
            data_copy(d, m).wait_recv()
            scale_copy(d, m).wait_recv()
    size = jnp.zeros((8, 128), f32)
    for k in range(2):
        ident = table[4 * z + 2 * c + k]
        for i in range(8):
            x = pair(7, k, i, ident)
            for d in range(2):
                m = 5 if PICK[d][5] == k else 6
                x = x + arrived(d, m, i)
            summed[k, pl.ds(32 * i, 32), :] = x
            size = size + fold(x * x, jnp.add)

    def norm_copy(stg, o):
        peer = {"rep": lax.rem(r + o, 16)} if stg == 0 else {"fsdp": lax.rem(f + o, 16)}
        return pltpu.make_async_remote_copy(
            src_ref=nsend.at[stg], dst_ref=nrecv.at[stg, o - 1], send_sem=n_ssem.at[stg], recv_sem=n_rsem.at[stg],
            device_id=peer, device_id_type=MESH,
        )

    def norm_all(stg):
        return pltpu.make_async_copy(nrecv.at[stg], nrecv.at[stg], n_rsem.at[stg])

    nsend[0] = size
    for o in range(1, 16):
        norm_copy(0, o).start()

    for load in loads[32:]:
        load.wait()
    for k in range(2):
        parts = split(summed[k])
        mats[2 * k] = gram_left(parts)
        mats[2 * k + 1] = gram_right(parts)

    norm_all(0).wait()
    for o in range(15):
        size = size + nrecv[0, o]
    nsend[1] = size
    for o in range(1, 16):
        norm_copy(1, o).start()
    norm_all(1).wait()
    for o in range(15):
        size = size + nrecv[1, o]
    norm_sq = jnp.sum(size, keepdims=True)
    clip = jnp.minimum(1.0, CLIP_NORM / (jnp.sqrt(norm_sq) + EPSILON))

    ident = eye()
    for k in range(2):
        for s in range(2):
            stats = left if s == 0 else right
            t = 2 * k + s
            a = stats[k] + (clip * clip) * mats[t] + EPSILON * ident
            zeta = 2.5 / jnp.sqrt(jnp.sum(a * a, keepdims=True))
            cur = zeta * a
            p = 1.25 * ident - 0.25 * cur
            roots[t] = jnp.sqrt(jnp.sqrt(zeta)) * p
            ps = split(p)
            ss = split(mm(ps, ps))
            qs = split(mm(ss, ss))
            mats[t] = mm(qs, split(cur))

    def sweep(i, carry):
        curs = [mats[t] for t in range(4)]
        pss = [split(1.25 * ident - 0.25 * cur) for cur in curs]
        for t in range(4):
            roots[t] = mm(split(roots[t]), pss[t])
        sss = [split(mm(p, p)) for p in pss]
        qss = [split(mm(s, s)) for s in sss]
        for t in range(4):
            mats[t] = mm(qss[t], split(curs[t]))
        return carry

    lax.fori_loop(0, ITERS - 2, sweep, 0)
    for t in range(4):
        p = 1.25 * ident - 0.25 * mats[t]
        roots[t] = mm(split(roots[t]), split(p))

    for k in range(2):
        g = clip * summed[k]
        sham = mm(split(mm(split(roots[2 * k]), split(g))), split(roots[2 * k + 1]))
        ada = g / (jnp.sqrt(accum[k] + g * g) + EPSILON)
        ada_size = jnp.sqrt(jnp.sum(ada * ada, keepdims=True))
        sham_size = jnp.sqrt(jnp.sum(sham * sham, keepdims=True))
        step = sham * (ada_size / (sham_size + EPSILON))
        steps[k] = step
        ag[4 * z + 2 * c + k] = (master[k] - STEP_RATE * step).astype(bf16)

    def slot_of(d, m, back):
        origin = at(-SIGN[d] * (AG_HOPS[m] - back))
        return 4 * origin + 2 * c + PICK[d][m]

    def ag_copy(d, m):
        slot = slot_of(d, m, 1)
        return pltpu.make_async_remote_copy(
            src_ref=ag.at[slot], dst_ref=ag.at[slot], send_sem=ag_ssem.at[d, m], recv_sem=ag_rsem.at[d, m],
            device_id=near(SIGN[d]), device_id_type=MESH,
        )

    def ag_recv(d, m):
        slot = slot_of(d, m, 0)
        return pltpu.make_async_remote_copy(
            src_ref=ag.at[slot], dst_ref=ag.at[slot], send_sem=ag_ssem.at[d, m], recv_sem=ag_rsem.at[d, m],
            device_id=near(SIGN[d]), device_id_type=MESH,
        )

    def mate_copy(n, slot):
        return pltpu.make_async_remote_copy(
            src_ref=ag.at[slot], dst_ref=ag.at[slot], send_sem=x_ssem.at[n], recv_sem=x_rsem.at[n],
            device_id=mate, device_id_type=MESH,
        )

    for m in range(2):
        for d in range(2):
            ag_copy(d, m).start()
    moves = []
    for k in range(2):
        moves.append((k, 4 * z + 2 * c + k))
        mate_copy(*moves[-1]).start()
    for m in range(7):
        for d in range(2):
            ag_recv(d, m).wait_recv()
            if m + 2 < 7:
                ag_copy(d, m + 2).start()
            moves.append((2 + 2 * m + d, slot_of(d, m, 0)))
            mate_copy(*moves[-1]).start()

    for move in moves:
        mate_copy(*move).wait_send()
        mate_copy(*move).wait_recv()
    for d in range(2):
        for m in range(7):
            ag_copy(d, m).wait_send()
            data_copy(d, m).wait_send()
            scale_copy(d, m).wait_send()
    for j in range(8):
        to_mate(j).wait_send()
    for stg in range(2):
        norm_all_sent = pltpu.make_async_copy(nrecv.at[stg], nrecv.at[stg], n_ssem.at[stg])
        norm_all_sent.wait()


def place(table, gath, steps_in, weights, steps, sems):
    copies = [pltpu.make_async_copy(steps_in, steps, sems.at[32])]
    for s in range(32):
        ident = table[s]
        top = pl.multiple_of((ident // 16) * W, W)
        lead = pl.multiple_of((ident % 16) * W, W)
        copies.append(
            pltpu.make_async_copy(gath.at[s], weights.at[pl.ds(top, W), pl.ds(lead, W)], sems.at[s])
        )
    for copy in copies:
        copy.start()
    for copy in copies:
        copy.wait()


def per_device(grad_parts, owner_table, left_stats, right_stats, accum, master):
    band = grad_parts[0]
    smem = pl.BlockSpec(memory_space=pltpu.SMEM)
    anyw = pl.BlockSpec(memory_space=pl.ANY)
    vmem = pl.BlockSpec(memory_space=pltpu.VMEM)
    tiles = (2, W, W)
    dma = pltpu.SemaphoreType.DMA
    steps, gath = pl.pallas_call(
        kernel,
        out_shape=(pltpu.VMEM(tiles, f32), pltpu.VMEM((32, W, W), bf16)),
        in_specs=[smem] + [pl.BlockSpec(memory_space=pltpu.HBM)] * 5,
        out_specs=(vmem, vmem),
        scratch_shapes=[
            pltpu.VMEM((32, W, W), bf16),
            pltpu.VMEM(tiles, f32),
            pltpu.VMEM(tiles, f32),
            pltpu.VMEM(tiles, f32),
            pltpu.VMEM(tiles, f32),
            pltpu.VMEM((8, 2 * W, W), bf16),
            pltpu.VMEM((8, 2 * W, W), bf16),
            pltpu.VMEM(tiles, f32),
            pltpu.VMEM((2, 7, W, W), i16),
            pltpu.VMEM((2, 7, 8, 128), f32),
            pltpu.VMEM((2, 7, W, W), i16),
            pltpu.VMEM((2, 7, 8, 128), f32),
            pltpu.VMEM(tiles, f32),
            pltpu.VMEM((2, 8, 128), f32),
            pltpu.VMEM((2, 15, 8, 128), f32),
            pltpu.VMEM((4, W, W), f32),
            pltpu.VMEM((4, W, W), f32),
            dma((5,)), dma((8,)), dma((8,)), dma((2, 7)), dma((2, 7)), dma((2, 7)), dma((2, 7)),
            dma((2,)), dma((2,)), dma((2, 7)), dma((2, 7)), dma((16,)), dma((16,)),
        ],
        compiler_params=pltpu.CompilerParams(
            collective_id=0, has_side_effects=True, vmem_limit_bytes=58 << 20
        ),
        name="shampoo",
    )(owner_table, band, left_stats, right_stats, accum, master)
    weights, steps = pl.pallas_call(
        place,
        out_shape=(
            jax.ShapeDtypeStruct(band.shape, bf16),
            jax.ShapeDtypeStruct(tiles, f32),
        ),
        in_specs=[smem, vmem, vmem],
        out_specs=(anyw, anyw),
        scratch_shapes=[dma((33,))],
        compiler_params=pltpu.CompilerParams(vmem_limit_bytes=16 << 20),
        name="place",
    )(owner_table, gath, steps)
    return (steps, weights)


def solution(mesh):
    return jax.shard_map(
        per_device,
        mesh=mesh,
        in_specs=(
            P("rep", "fsdp", None),
            P(),
            P(("fsdp", "rep"), None, None),
            P(("fsdp", "rep"), None, None),
            P(("fsdp", "rep"), None, None),
            P(("fsdp", "rep"), None, None),
        ),
        out_specs=(P(("fsdp", "rep"), None, None), P("fsdp", None)),
        check_vma=False,
    )
```

```python
import functools
import jax
import jax.numpy as jnp
from jax import lax
from jax.experimental import pallas as pl
from jax.experimental.pallas import tpu as pltpu
from jax.sharding import PartitionSpec as P

ITERS = 8
EPSILON = 1e-06
STEP_RATE = 0.2
CLIP_NORM = 1.0
W = 256
LEVELS = 32767.0
TINY = 1e-30
f32, bf16, i16 = jnp.float32, jnp.bfloat16, jnp.int16
MESH = pl.DeviceIdType.MESH

RS_ORDER = ((4, 0), (3, 1), (3, 0), (2, 1), (2, 0), (1, 1), (1, 0), (0, 0))
AG_ORDER = ((1, 0), (1, 1), (2, 0), (2, 1), (3, 0), (3, 1), (4, 0))


def split(x):
    high = x.astype(bf16)
    return high, (x - high.astype(f32)).astype(bf16)


def dot(a, b):
    return jnp.dot(a, b, preferred_element_type=f32)


def mm(a, b):
    return dot(a[0], b[0]) + (dot(a[0], b[1]) + dot(a[1], b[0]))


def gram_left(a):
    def one(u, v):
        return lax.dot_general(u, v, (((1,), (1,)), ((), ())), preferred_element_type=f32)

    return one(a[0], a[0]) + (one(a[0], a[1]) + one(a[1], a[0]))


def gram_right(a):
    def one(u, v):
        return lax.dot_general(u, v, (((0,), (0,)), ((), ())), preferred_element_type=f32)

    return one(a[0], a[0]) + (one(a[0], a[1]) + one(a[1], a[0]))


def eye():
    rows = lax.broadcasted_iota(jnp.int32, (W, W), 0)
    return (rows == lax.broadcasted_iota(jnp.int32, (W, W), 1)).astype(f32)


def spread(scale):
    return jnp.broadcast_to(jnp.concatenate([scale, scale], axis=1), (32, W))


def fold(x, op):
    parts = [x[8 * i : 8 * i + 8, :] for i in range(4)]
    both = op(op(parts[0], parts[1]), op(parts[2], parts[3]))
    return op(both[:, :128], both[:, 128:])


def kernel(
    table, band_h, left_h, right_h, accum_h, master_h,
    steps, ag,
    band, left, right, accum, master,
    stage, sib, total, sendq, sends, recvq, recvs, summed, nsend, nrecv,
    mats, roots,
    in_sem, sib_ssem, sib_rsem, q_ssem, q_rsem, s_ssem, s_rsem,
    n_ssem, n_rsem, ag_ssem, ag_rsem, x_ssem, x_rsem, own_rsem,
):
    f = lax.axis_index("fsdp")
    r = lax.axis_index("rep")
    z = r // 2
    c = r - 2 * z
    mate = {"rep": r + 1 - 2 * c}
    once = jnp.minimum(r + 1, 1)

    def block(work):
        def body(i, carry):
            work()
            return carry

        lax.fori_loop(0, once, body, 0)

    chips = 8

    way = 2 * c - 1

    def chip(hops):
        return lax.rem(z + way * hops + chips, chips)

    def core(other):
        return 1 - c if other else c

    loads = [
        pltpu.make_async_copy(
            band_h.at[pl.ds(W * (t // 16), W), pl.ds(W * (t % 16), W)], band.at[t], in_sem.at[0]
        )
        for t in range(32)
    ] + [
        pltpu.make_async_copy(left_h, left, in_sem.at[1]),
        pltpu.make_async_copy(right_h, right, in_sem.at[2]),
        pltpu.make_async_copy(accum_h, accum, in_sem.at[3]),
        pltpu.make_async_copy(master_h, master, in_sem.at[4]),
    ]
    for load in loads:
        load.start()
    barrier = pltpu.get_barrier_semaphore()
    for o in range(1, 16):
        pl.semaphore_signal(barrier, 1, device_id={"rep": lax.rem(r + o, 16)}, device_id_type=MESH)
        pl.semaphore_signal(barrier, 1, device_id={"fsdp": lax.rem(f + o, 16)}, device_id_type=MESH)

    pltpu.make_async_copy(band, band, in_sem.at[0]).wait()

    def to_mate(j):
        return pltpu.make_async_remote_copy(
            src_ref=stage.at[j], dst_ref=sib.at[j], send_sem=sib_ssem, recv_sem=sib_rsem.at[j],
            device_id=mate, device_id_type=MESH,
        )

    def fill(j):
        hops, other = RS_ORDER[j]
        for k in range(2):
            stage[j, pl.ds(k * W, W), :] = band[table[4 * chip(-hops) + 2 * core(1 - other) + k]]

    for j in range(8):
        fill(j)
        if j == 0:
            pl.semaphore_wait(barrier, 30)
        to_mate(j).start()

    def pair(j, k, i, ident):
        own = band[ident, pl.ds(32 * i, 32), :].astype(f32)
        return own + sib[j, pl.ds(k * W + 32 * i, 32), :].astype(f32)

    def arrived(j, k, i):
        return recvq[j, k, pl.ds(32 * i, 32), :].astype(f32) * spread(recvs[j, k])

    def ahead(j):
        return {"rep": 2 * chip(1) + (core(RS_ORDER[j][1]) if RS_ORDER[j][0] == 1 else c)}

    def data_copy(j, k):
        return pltpu.make_async_remote_copy(
            src_ref=sendq.at[j, k], dst_ref=recvq.at[j, k], send_sem=q_ssem, recv_sem=q_rsem.at[j, k],
            device_id=ahead(j), device_id_type=MESH,
        )

    def scale_copy(j, k):
        return pltpu.make_async_remote_copy(
            src_ref=sends.at[j, k], dst_ref=recvs.at[j, k], send_sem=s_ssem.at[j, k], recv_sem=s_rsem.at[j, k],
            device_id=ahead(j), device_id_type=MESH,
        )

    def message(j, k):
        hops, other = RS_ORDER[j]
        ident = table[4 * chip(hops) + 2 * core(other) + k]
        if j >= 2:
            data_copy(j - 2, k).wait_recv()
            scale_copy(j - 2, k).wait_recv()
        most = jnp.full((8, 128), TINY, f32)
        for i in range(8):
            x = pair(j, k, i, ident)
            if j >= 2:
                x = x + arrived(j - 2, k, i)
            total[k, pl.ds(32 * i, 32), :] = x
            most = jnp.maximum(most, fold(jnp.abs(x), jnp.maximum))
        most = jnp.max(most, axis=0, keepdims=True)
        sends[j, k] = most * (1.0 / LEVELS)
        inverse = spread(LEVELS / most)
        for i in range(8):
            x = total[k, pl.ds(32 * i, 32), :] * inverse
            sendq[j, k, pl.ds(32 * i, 32), :] = jnp.round(x).astype(jnp.int32).astype(i16)
        data_copy(j, k).start()
        scale_copy(j, k).start()

    for j in range(7):
        to_mate(j).wait_recv()
        for k in range(2):
            message(j, k)
    to_mate(7).wait_recv()
    size = jnp.zeros((8, 128), f32)
    for k in range(2):
        ident = table[4 * z + 2 * c + k]
        for j in (5, 6):
            data_copy(j, k).wait_recv()
            scale_copy(j, k).wait_recv()
        for i in range(8):
            x = pair(7, k, i, ident) + arrived(5, k, i) + arrived(6, k, i)
            summed[k, pl.ds(32 * i, 32), :] = x
            size = size + fold(x * x, jnp.add)

    def norm_copy(stg, o):
        peer = {"rep": lax.rem(r + o, 16)} if stg == 0 else {"fsdp": lax.rem(f + o, 16)}
        return pltpu.make_async_remote_copy(
            src_ref=nsend.at[stg], dst_ref=nrecv.at[stg, o - 1], send_sem=n_ssem.at[stg], recv_sem=n_rsem.at[stg],
            device_id=peer, device_id_type=MESH,
        )

    def norm_all(stg):
        return pltpu.make_async_copy(nrecv.at[stg], nrecv.at[stg], n_rsem.at[stg])

    nsend[0] = size
    for o in range(1, 16):
        norm_copy(0, o).start()

    for load in loads[32:]:
        load.wait()

    def left_grams():
        for k in range(2):
            mats[2 * k] = gram_left(split(summed[k]))

    def right_grams():
        for k in range(2):
            mats[2 * k + 1] = gram_right(split(summed[k]))

    block(left_grams)
    norm_all(0).wait()
    for o in range(15):
        size = size + nrecv[0, o]
    nsend[1] = size
    for o in range(1, 16):
        norm_copy(1, o).start()
    block(right_grams)
    norm_all(1).wait()
    for o in range(15):
        size = size + nrecv[1, o]
    norm_sq = jnp.sum(size, keepdims=True)
    clip = jnp.minimum(1.0, CLIP_NORM / (jnp.sqrt(norm_sq) + EPSILON))

    ident = eye()
    for k in range(2):
        for s in range(2):
            stats = left if s == 0 else right
            t = 2 * k + s
            a = stats[k] + (clip * clip) * mats[t] + EPSILON * ident
            zeta = 2.5 / jnp.sqrt(jnp.sum(a * a, keepdims=True))
            cur = zeta * a
            p = 1.25 * ident - 0.25 * cur
            roots[t] = jnp.sqrt(jnp.sqrt(zeta)) * p
            ps = split(p)
            ss = split(mm(ps, ps))
            mats[t] = mm(split(mm(ss, split(cur))), ss)

    for _ in range(ITERS - 2):
        curs = [mats[t] for t in range(4)]
        pss = [split(1.25 * ident - 0.25 * cur) for cur in curs]
        sss = [split(mm(p, p)) for p in pss]
        for t in range(4):
            roots[t] = mm(split(roots[t]), pss[t])
        uss = [split(mm(p, split(cur))) for p, cur in zip(sss, curs)]
        for t in range(4):
            mats[t] = mm(uss[t], sss[t])

    def last_roots(k):
        for t in (2 * k, 2 * k + 1):
            p = 1.25 * ident - 0.25 * mats[t]
            roots[t] = mm(split(roots[t]), split(p))

    def finish(k):
        g = clip * summed[k]
        sham = mm(split(mm(split(roots[2 * k]), split(g))), split(roots[2 * k + 1]))
        ada = g / (jnp.sqrt(accum[k] + g * g) + EPSILON)
        ada_size = jnp.sqrt(jnp.sum(ada * ada, keepdims=True))
        sham_size = jnp.sqrt(jnp.sum(sham * sham, keepdims=True))
        step = sham * (ada_size / (sham_size + EPSILON))
        steps[k] = step
        ag[4 * z + 2 * c + k] = (master[k] - STEP_RATE * step).astype(bf16)

    def ag_copy(i, k, back=1):
        hops, other = AG_ORDER[i]
        slot = 4 * chip(back - hops) + 2 * core(other) + k
        return pltpu.make_async_remote_copy(
            src_ref=ag.at[slot], dst_ref=ag.at[slot], send_sem=ag_ssem, recv_sem=ag_rsem.at[i, k],
            device_id={"rep": 2 * chip(1) + c}, device_id_type=MESH,
        )

    def share(i, k):
        hops, other = AG_ORDER[i]
        slot = 4 * chip(-hops) + 2 * core(other) + k
        return pltpu.make_async_remote_copy(
            src_ref=ag.at[slot], dst_ref=ag.at[slot], send_sem=x_ssem, recv_sem=x_rsem,
            device_id=mate, device_id_type=MESH,
        )

    def own_share(k):
        slot = 4 * z + 2 * c + k
        return pltpu.make_async_remote_copy(
            src_ref=ag.at[slot], dst_ref=ag.at[slot], send_sem=x_ssem, recv_sem=own_rsem.at[k],
            device_id=mate, device_id_type=MESH,
        )

    def own_out(k):
        ag_copy(0, k).start()
        own_share(k).start()

    def mate_out(k):
        own_share(k).wait_recv()
        ag_copy(1, k).start()

    last_roots(0)
    finish(0)
    own_out(0)
    block(lambda: last_roots(1))
    mate_out(0)
    block(lambda: finish(1))
    own_out(1)
    mate_out(1)
    for i in range(7):
        for k in range(2):
            ag_copy(i, k, 0).wait_recv()
            if i + 2 < 7:
                ag_copy(i + 2, k).start()
            share(i, k).start()

    def drain(ref, sem):
        pltpu.make_async_copy(ref, ref, sem).wait()

    drain(stage, sib_ssem)
    drain(sendq, q_ssem)
    drain(ag.at[pl.ds(0, 14)], ag_ssem)
    drain(ag.at[pl.ds(0, 16)], x_ssem)
    for j in range(7):
        for k in range(2):
            scale_copy(j, k).wait_send()
    for stg in range(2):
        drain(nrecv.at[stg], n_ssem.at[stg])
    drain(ag.at[pl.ds(0, 14)], x_rsem)


def place(table, gath, steps_in, weights, steps, sems):
    for s in range(32):
        ident = table[s]
        top = pl.multiple_of((ident // 16) * W, W)
        lead = pl.multiple_of((ident % 16) * W, W)
        pltpu.make_async_copy(gath.at[s], weights.at[pl.ds(top, W), pl.ds(lead, W)], sems.at[0]).start()
    keep = pltpu.make_async_copy(steps_in, steps, sems.at[1])
    keep.start()
    pltpu.make_async_copy(gath, gath, sems.at[0]).wait()
    keep.wait()


def per_device(grad_parts, owner_table, left_stats, right_stats, accum, master):
    band = grad_parts[0]
    smem = pl.BlockSpec(memory_space=pltpu.SMEM)
    anyw = pl.BlockSpec(memory_space=pl.ANY)
    vmem = pl.BlockSpec(memory_space=pltpu.VMEM)
    tiles = (2, W, W)
    dma = pltpu.SemaphoreType.DMA
    steps, gath = pl.pallas_call(
        kernel,
        out_shape=(pltpu.VMEM(tiles, f32), pltpu.VMEM((32, W, W), bf16)),
        in_specs=[smem] + [pl.BlockSpec(memory_space=pltpu.HBM)] * 5,
        out_specs=(vmem, vmem),
        scratch_shapes=[
            pltpu.VMEM((32, W, W), bf16),
            pltpu.VMEM(tiles, f32),
            pltpu.VMEM(tiles, f32),
            pltpu.VMEM(tiles, f32),
            pltpu.VMEM(tiles, f32),
            pltpu.VMEM((8, 2 * W, W), bf16),
            pltpu.VMEM((8, 2 * W, W), bf16),
            pltpu.VMEM(tiles, f32),
            pltpu.VMEM((7, 2, W, W), i16),
            pltpu.VMEM((7, 2, 1, 128), f32),
            pltpu.VMEM((7, 2, W, W), i16),
            pltpu.VMEM((7, 2, 1, 128), f32),
            pltpu.VMEM(tiles, f32),
            pltpu.VMEM((2, 8, 128), f32),
            pltpu.VMEM((2, 15, 8, 128), f32),
            pltpu.VMEM((4, W, W), f32),
            pltpu.VMEM((4, W, W), f32),
            dma((5,)), dma, dma((8,)), dma, dma((7, 2)), dma((7, 2)), dma((7, 2)),
            dma((2,)), dma((2,)), dma, dma((7, 2)), dma, dma, dma((2,)),
        ],
        compiler_params=pltpu.CompilerParams(
            collective_id=0, has_side_effects=True, vmem_limit_bytes=58 << 20
        ),
        name="shampoo",
    )(owner_table, band, left_stats, right_stats, accum, master)
    weights, steps = pl.pallas_call(
        place,
        out_shape=(
            jax.ShapeDtypeStruct(band.shape, bf16),
            jax.ShapeDtypeStruct(tiles, f32),
        ),
        in_specs=[smem, vmem, vmem],
        out_specs=(anyw, anyw),
        scratch_shapes=[dma((2,))],
        compiler_params=pltpu.CompilerParams(vmem_limit_bytes=16 << 20),
        name="place",
    )(owner_table, gath, steps)
    return (steps, weights)


def solution(mesh):
    return jax.shard_map(
        per_device,
        mesh=mesh,
        in_specs=(
            P("rep", "fsdp", None),
            P(),
            P(("fsdp", "rep"), None, None),
            P(("fsdp", "rep"), None, None),
            P(("fsdp", "rep"), None, None),
            P(("fsdp", "rep"), None, None),
        ),
        out_specs=(P(("fsdp", "rep"), None, None), P("fsdp", None)),
        check_vma=False,
    )
```

```python
import functools
import jax
import jax.numpy as jnp
from jax import lax
from jax.experimental import pallas as pl
from jax.experimental.pallas import tpu as pltpu
from jax.sharding import PartitionSpec as P

ITERS = 8
EPSILON = 1e-06
STEP_RATE = 0.2
CLIP_NORM = 1.0
W = 256
LEVELS = 32767.0
TINY = 1e-30
f32, bf16, i16 = jnp.float32, jnp.bfloat16, jnp.int16
MESH = pl.DeviceIdType.MESH

RS_ORDER = ((4, 0), (3, 1), (3, 0), (2, 1), (2, 0), (1, 1), (1, 0), (0, 0))
AG_ORDER = ((1, 0), (1, 1), (2, 0), (2, 1), (3, 0), (3, 1), (4, 0))


def split(x):
    high = x.astype(bf16)
    return high, (x - high.astype(f32)).astype(bf16)


def dot(a, b):
    return jnp.dot(a, b, preferred_element_type=f32)


def mm(a, b):
    return dot(a[0], b[0]) + (dot(a[0], b[1]) + dot(a[1], b[0]))


def gram_left(a):
    def one(u, v):
        return lax.dot_general(u, v, (((1,), (1,)), ((), ())), preferred_element_type=f32)

    return one(a[0], a[0]) + (one(a[0], a[1]) + one(a[1], a[0]))


def gram_right(a):
    def one(u, v):
        return lax.dot_general(u, v, (((0,), (0,)), ((), ())), preferred_element_type=f32)

    return one(a[0], a[0]) + (one(a[0], a[1]) + one(a[1], a[0]))


def eye():
    rows = lax.broadcasted_iota(jnp.int32, (W, W), 0)
    return (rows == lax.broadcasted_iota(jnp.int32, (W, W), 1)).astype(f32)


def spread(scale):
    return jnp.broadcast_to(jnp.concatenate([scale, scale], axis=1), (32, W))


def fold(x, op):
    parts = [x[8 * i : 8 * i + 8, :] for i in range(4)]
    both = op(op(parts[0], parts[1]), op(parts[2], parts[3]))
    return op(both[:, :128], both[:, 128:])


def kernel(
    table_h, band_h, left_h, right_h, accum_h, master_h,
    steps, ag,
    table, band, left, right, accum, master,
    stage, sib, total, sendq, sends, recvq, recvs, summed, nsend, nrecv,
    mats, roots,
    in_sem, near_sem, sib_ssem, sib_rsem, q_ssem, q_rsem, s_ssem, s_rsem,
    n_ssem, n_rsem, ag_ssem, ag_rsem, x_ssem, x_rsem, own_rsem,
):
    f = lax.axis_index("fsdp")
    r = lax.axis_index("rep")
    z = r // 2
    c = r - 2 * z
    mate = {"rep": r + 1 - 2 * c}
    once = jnp.minimum(r + 1, 1)

    def block(work):
        def body(i, carry):
            work()
            return carry

        lax.fori_loop(0, once, body, 0)

    chips = 8

    way = 2 * c - 1

    def chip(hops):
        return lax.rem(z + way * hops + chips, chips)

    def core(other):
        return 1 - c if other else c

    loads = [
        pltpu.make_async_copy(
            band_h.at[pl.ds(W * (t // 16), W), pl.ds(W * (t % 16), W)], band.at[t], in_sem.at[0]
        )
        for t in range(32)
    ] + [
        pltpu.make_async_copy(left_h, left, in_sem.at[1]),
        pltpu.make_async_copy(right_h, right, in_sem.at[2]),
        pltpu.make_async_copy(accum_h, accum, in_sem.at[3]),
        pltpu.make_async_copy(master_h, master, in_sem.at[4]),
    ]
    row = f - lax.rem(f, 4)
    beside = [
        {"fsdp": row + lax.rem(f + 1, 4)},
        {"fsdp": row + lax.rem(f + 3, 4)},
        {"fsdp": lax.rem(f + 4, 16)},
        {"fsdp": lax.rem(f + 12, 16)},
    ]
    ring = [mate, {"rep": 2 * chip(1) + c}, {"rep": 2 * chip(-1) + c}, {"rep": 2 * chip(1) + 1 - c}]
    barrier = pltpu.get_barrier_semaphore()
    for peer in ring + beside:
        pl.semaphore_signal(barrier, 1, device_id=peer, device_id_type=MESH)

    def tell(turn):
        for peer in beside:
            pl.semaphore_signal(near_sem.at[turn], 1, device_id=peer, device_id_type=MESH)

    fetch_table = pltpu.make_async_copy(table_h, table, in_sem.at[5])
    fetch_table.start()
    for load in loads[:32]:
        load.start()
    fetch_table.wait()
    pltpu.make_async_copy(band, band, in_sem.at[0]).wait()
    for load in loads[32:]:
        load.start()

    def to_mate(j):
        return pltpu.make_async_remote_copy(
            src_ref=stage.at[j], dst_ref=sib.at[j], send_sem=sib_ssem, recv_sem=sib_rsem.at[j],
            device_id=mate, device_id_type=MESH,
        )

    def fill(j):
        hops, other = RS_ORDER[j]
        for k in range(2):
            stage[j, pl.ds(k * W, W), :] = band[table[4 * chip(-hops) + 2 * core(1 - other) + k]]

    for j in range(8):
        fill(j)
        if j == 0:
            pl.semaphore_wait(barrier, 8)
        to_mate(j).start()

    def pair(j, k, i, ident):
        own = band[ident, pl.ds(32 * i, 32), :].astype(f32)
        return own + sib[j, pl.ds(k * W + 32 * i, 32), :].astype(f32)

    def arrived(j, k, i):
        return recvq[j, k, pl.ds(32 * i, 32), :].astype(f32) * spread(recvs[j, k])

    def ahead(j):
        return {"rep": 2 * chip(1) + (core(RS_ORDER[j][1]) if RS_ORDER[j][0] == 1 else c)}

    def data_copy(j, k):
        return pltpu.make_async_remote_copy(
            src_ref=sendq.at[j, k], dst_ref=recvq.at[j, k], send_sem=q_ssem, recv_sem=q_rsem.at[j, k],
            device_id=ahead(j), device_id_type=MESH,
        )

    def scale_copy(j, k):
        return pltpu.make_async_remote_copy(
            src_ref=sends.at[j, k], dst_ref=recvs.at[j, k], send_sem=s_ssem.at[j, k], recv_sem=s_rsem.at[j, k],
            device_id=ahead(j), device_id_type=MESH,
        )

    def message(j, k):
        hops, other = RS_ORDER[j]
        ident = table[4 * chip(hops) + 2 * core(other) + k]
        if j >= 2:
            data_copy(j - 2, k).wait_recv()
            scale_copy(j - 2, k).wait_recv()
        most = jnp.full((8, 128), TINY, f32)
        for i in range(8):
            x = pair(j, k, i, ident)
            if j >= 2:
                x = x + arrived(j - 2, k, i)
            total[k, pl.ds(32 * i, 32), :] = x
            most = jnp.maximum(most, fold(jnp.abs(x), jnp.maximum))
        most = jnp.max(most, axis=0, keepdims=True)
        sends[j, k] = most * (1.0 / LEVELS)
        inverse = spread(LEVELS / most)
        for i in range(8):
            x = total[k, pl.ds(32 * i, 32), :] * inverse
            sendq[j, k, pl.ds(32 * i, 32), :] = jnp.round(x).astype(jnp.int32).astype(i16)
        data_copy(j, k).start()
        scale_copy(j, k).start()

    tell(0)
    for j in range(7):
        to_mate(j).wait_recv()
        for k in range(2):
            message(j, k)
        if j in (2, 4, 6):
            turn = j // 2 - 1
            pl.semaphore_wait(near_sem.at[turn], 4)
            if turn < 2:
                tell(turn + 1)
    to_mate(7).wait_recv()
    size = jnp.zeros((8, 128), f32)
    for k in range(2):
        ident = table[4 * z + 2 * c + k]
        for j in (5, 6):
            data_copy(j, k).wait_recv()
            scale_copy(j, k).wait_recv()
        for i in range(8):
            x = pair(7, k, i, ident) + arrived(5, k, i) + arrived(6, k, i)
            summed[k, pl.ds(32 * i, 32), :] = x
            size = size + fold(x * x, jnp.add)

    def norm_copy(stg, o):
        peer = {"rep": lax.rem(r + o, 16)} if stg == 0 else {"fsdp": lax.rem(f + o, 16)}
        return pltpu.make_async_remote_copy(
            src_ref=nsend.at[stg], dst_ref=nrecv.at[stg, o - 1], send_sem=n_ssem.at[stg], recv_sem=n_rsem.at[stg],
            device_id=peer, device_id_type=MESH,
        )

    def norm_all(stg):
        return pltpu.make_async_copy(nrecv.at[stg], nrecv.at[stg], n_rsem.at[stg])

    nsend[0] = size
    for o in range(1, 16):
        norm_copy(0, o).start()

    for load in loads[32:]:
        load.wait()

    def left_grams():
        for k in range(2):
            mats[2 * k] = gram_left(split(summed[k]))

    def right_grams():
        for k in range(2):
            mats[2 * k + 1] = gram_right(split(summed[k]))

    block(left_grams)
    norm_all(0).wait()
    for o in range(15):
        size = size + nrecv[0, o]
    nsend[1] = size
    for o in range(1, 16):
        norm_copy(1, o).start()
    block(right_grams)
    norm_all(1).wait()
    for o in range(15):
        size = size + nrecv[1, o]
    norm_sq = jnp.sum(size, keepdims=True)
    clip = jnp.minimum(1.0, CLIP_NORM / (jnp.sqrt(norm_sq) + EPSILON))

    ident = eye()
    fourths, factors = [], []

    def advance(k, left_factor, right_factor):
        roots[k] = mm(split(mm(left_factor, split(roots[k]))), right_factor)

    for k in range(2):
        for s in range(2):
            stats = left if s == 0 else right
            t = 2 * k + s
            a = stats[k] + (clip * clip) * mats[t] + EPSILON * ident
            zeta = 2.5 / jnp.sqrt(jnp.sum(a * a, keepdims=True))
            cur = zeta * a
            p = 1.25 * ident - 0.25 * cur
            fourths.append(jnp.sqrt(jnp.sqrt(zeta)))
            ps = split(p)
            factors.append(ps)
            ss = split(mm(ps, ps))
            mats[t] = mm(split(mm(ss, split(cur))), ss)

    for k in range(2):
        roots[k] = (clip * fourths[2 * k] * fourths[2 * k + 1]) * summed[k]
        advance(k, factors[2 * k], factors[2 * k + 1])

    for _ in range(ITERS - 2):
        curs = [mats[t] for t in range(4)]
        pss = [split(1.25 * ident - 0.25 * cur) for cur in curs]
        sss = [split(mm(p, p)) for p in pss]
        for k in range(2):
            advance(k, pss[2 * k], pss[2 * k + 1])
        uss = [split(mm(p, split(cur))) for p, cur in zip(sss, curs)]
        for t in range(4):
            mats[t] = mm(uss[t], sss[t])

    def last_factors(k):
        advance(k, *(split(1.25 * ident - 0.25 * mats[t]) for t in (2 * k, 2 * k + 1)))

    def finish(k):
        g = clip * summed[k]
        sham = roots[k]
        ada = g / (jnp.sqrt(accum[k] + g * g) + EPSILON)
        ada_size = jnp.sqrt(jnp.sum(ada * ada, keepdims=True))
        sham_size = jnp.sqrt(jnp.sum(sham * sham, keepdims=True))
        step = sham * (ada_size / (sham_size + EPSILON))
        steps[k] = step
        ag[4 * z + 2 * c + k] = (master[k] - STEP_RATE * step).astype(bf16)

    def ag_copy(i, k, back=1):
        hops, other = AG_ORDER[i]
        slot = 4 * chip(back - hops) + 2 * core(other) + k
        return pltpu.make_async_remote_copy(
            src_ref=ag.at[slot], dst_ref=ag.at[slot], send_sem=ag_ssem, recv_sem=ag_rsem.at[i, k],
            device_id={"rep": 2 * chip(1) + c}, device_id_type=MESH,
        )

    def share(i, k):
        hops, other = AG_ORDER[i]
        slot = 4 * chip(-hops) + 2 * core(other) + k
        return pltpu.make_async_remote_copy(
            src_ref=ag.at[slot], dst_ref=ag.at[slot], send_sem=x_ssem, recv_sem=x_rsem,
            device_id=mate, device_id_type=MESH,
        )

    def own_share(k):
        slot = 4 * z + 2 * c + k
        return pltpu.make_async_remote_copy(
            src_ref=ag.at[slot], dst_ref=ag.at[slot], send_sem=x_ssem, recv_sem=own_rsem.at[k],
            device_id=mate, device_id_type=MESH,
        )

    def own_out(k):
        ag_copy(0, k).start()
        own_share(k).start()

    def mate_out(k):
        own_share(k).wait_recv()
        ag_copy(1, k).start()

    last_factors(0)
    finish(0)
    own_out(0)
    block(lambda: last_factors(1))
    mate_out(0)
    block(lambda: finish(1))
    own_out(1)
    mate_out(1)
    for i in range(7):
        for k in range(2):
            ag_copy(i, k, 0).wait_recv()
            if i + 2 < 7:
                ag_copy(i + 2, k).start()
            share(i, k).start()

    def drain(ref, sem):
        pltpu.make_async_copy(ref, ref, sem).wait()

    drain(stage, sib_ssem)
    drain(sendq, q_ssem)
    drain(ag.at[pl.ds(0, 14)], ag_ssem)
    drain(ag.at[pl.ds(0, 16)], x_ssem)
    for j in range(7):
        for k in range(2):
            scale_copy(j, k).wait_send()
    for stg in range(2):
        drain(nrecv.at[stg], n_ssem.at[stg])
    drain(ag.at[pl.ds(0, 14)], x_rsem)


def place(table, gath, steps_in, weights, steps, sems):
    for s in range(32):
        ident = table[s]
        top = pl.multiple_of((ident // 16) * W, W)
        lead = pl.multiple_of((ident % 16) * W, W)
        pltpu.make_async_copy(gath.at[s], weights.at[pl.ds(top, W), pl.ds(lead, W)], sems.at[0]).start()
    keep = pltpu.make_async_copy(steps_in, steps, sems.at[1])
    keep.start()
    pltpu.make_async_copy(gath, gath, sems.at[0]).wait()
    keep.wait()


def per_device(grad_parts, owner_table, left_stats, right_stats, accum, master):
    band = grad_parts[0]
    smem = pl.BlockSpec(memory_space=pltpu.SMEM)
    anyw = pl.BlockSpec(memory_space=pl.ANY)
    vmem = pl.BlockSpec(memory_space=pltpu.VMEM)
    tiles = (2, W, W)
    dma = pltpu.SemaphoreType.DMA
    steps, gath = pl.pallas_call(
        kernel,
        out_shape=(pltpu.VMEM(tiles, f32), pltpu.VMEM((32, W, W), bf16)),
        in_specs=[pl.BlockSpec(memory_space=pltpu.HBM)] * 6,
        out_specs=(vmem, vmem),
        scratch_shapes=[
            pltpu.SMEM((32,), jnp.int32),
            pltpu.VMEM((32, W, W), bf16),
            pltpu.VMEM(tiles, f32),
            pltpu.VMEM(tiles, f32),
            pltpu.VMEM(tiles, f32),
            pltpu.VMEM(tiles, f32),
            pltpu.VMEM((8, 2 * W, W), bf16),
            pltpu.VMEM((8, 2 * W, W), bf16),
            pltpu.VMEM(tiles, f32),
            pltpu.VMEM((7, 2, W, W), i16),
            pltpu.VMEM((7, 2, 1, 128), f32),
            pltpu.VMEM((7, 2, W, W), i16),
            pltpu.VMEM((7, 2, 1, 128), f32),
            pltpu.VMEM(tiles, f32),
            pltpu.VMEM((2, 8, 128), f32),
            pltpu.VMEM((2, 15, 8, 128), f32),
            pltpu.VMEM((4, W, W), f32),
            pltpu.VMEM(tiles, f32),
            dma((6,)), pltpu.SemaphoreType.REGULAR((3,)), dma, dma((8,)), dma, dma((7, 2)), dma((7, 2)), dma((7, 2)),
            dma((2,)), dma((2,)), dma, dma((7, 2)), dma, dma, dma((2,)),
        ],
        compiler_params=pltpu.CompilerParams(
            collective_id=0, has_side_effects=True, vmem_limit_bytes=58 << 20
        ),
        name="shampoo",
    )(owner_table, band, left_stats, right_stats, accum, master)
    weights, steps = pl.pallas_call(
        place,
        out_shape=(
            jax.ShapeDtypeStruct(band.shape, bf16),
            jax.ShapeDtypeStruct(tiles, f32),
        ),
        in_specs=[smem, vmem, vmem],
        out_specs=(anyw, anyw),
        scratch_shapes=[dma((2,))],
        compiler_params=pltpu.CompilerParams(vmem_limit_bytes=16 << 20),
        name="place",
    )(owner_table, gath, steps)
    return (steps, weights)


def solution(mesh):
    return jax.shard_map(
        per_device,
        mesh=mesh,
        in_specs=(
            P("rep", "fsdp", None),
            P(),
            P(("fsdp", "rep"), None, None),
            P(("fsdp", "rep"), None, None),
            P(("fsdp", "rep"), None, None),
            P(("fsdp", "rep"), None, None),
        ),
        out_specs=(P(("fsdp", "rep"), None, None), P("fsdp", None)),
        check_vma=False,
    )
```

```python
import functools
import jax
import jax.numpy as jnp
from jax import lax
from jax.experimental import pallas as pl
from jax.experimental.pallas import tpu as pltpu
from jax.sharding import PartitionSpec as P

ITERS = 8
EPSILON = 1e-06
STEP_RATE = 0.2
CLIP_NORM = 1.0
W = 256
LEVELS = 32767.0
TINY = 1e-30
f32, bf16, i16 = jnp.float32, jnp.bfloat16, jnp.int16
MESH = pl.DeviceIdType.MESH

RS_ORDER = ((4, 0), (3, 1), (3, 0), (2, 1), (2, 0), (1, 1), (1, 0), (0, 0))
AG_ORDER = ((1, 0), (1, 1), (2, 0), (2, 1), (3, 0), (3, 1), (4, 0))


def split(x):
    high = x.astype(bf16)
    return high, (x - high.astype(f32)).astype(bf16)


def dot(a, b):
    return jnp.dot(a, b, preferred_element_type=f32)


def mm(a, b):
    return dot(a[0], b[0]) + (dot(a[0], b[1]) + dot(a[1], b[0]))


def gram_left(a):
    def one(u, v):
        return lax.dot_general(u, v, (((1,), (1,)), ((), ())), preferred_element_type=f32)

    return one(a[0], a[0]) + (one(a[0], a[1]) + one(a[1], a[0]))


def gram_right(a):
    def one(u, v):
        return lax.dot_general(u, v, (((0,), (0,)), ((), ())), preferred_element_type=f32)

    return one(a[0], a[0]) + (one(a[0], a[1]) + one(a[1], a[0]))


def eye():
    rows = lax.broadcasted_iota(jnp.int32, (W, W), 0)
    return (rows == lax.broadcasted_iota(jnp.int32, (W, W), 1)).astype(f32)


def spread(scale):
    return jnp.broadcast_to(jnp.concatenate([scale, scale], axis=1), (32, W))


def fold(x, op):
    parts = [x[8 * i : 8 * i + 8, :] for i in range(4)]
    both = op(op(parts[0], parts[1]), op(parts[2], parts[3]))
    return op(both[:, :128], both[:, 128:])


def kernel(
    table_h, band_h, left_h, right_h, accum_h, master_h,
    steps, ag,
    table, band, left, right, accum, master,
    stage, sib, total, sendq, sends, recvq, recvs, summed, nsend, nrecv,
    mats, roots, frob,
    in_sem, near_sem, sib_ssem, sib_rsem, q_ssem, q_rsem, s_ssem, s_rsem,
    n_ssem, n_rsem, ag_ssem, ag_rsem, x_ssem, x_rsem, own_rsem,
):
    f = lax.axis_index("fsdp")
    r = lax.axis_index("rep")
    z = r // 2
    c = r - 2 * z
    mate = {"rep": r + 1 - 2 * c}
    once = jnp.minimum(r + 1, 1)

    def block(work):
        def body(i, carry):
            work()
            return carry

        lax.fori_loop(0, once, body, 0)

    chips = 8

    way = 2 * c - 1

    def chip(hops):
        return lax.rem(z + way * hops + chips, chips)

    def core(other):
        return 1 - c if other else c

    loads = [
        pltpu.make_async_copy(
            band_h.at[pl.ds(W * (t // 16), W), pl.ds(W * (t % 16), W)], band.at[t], in_sem.at[0]
        )
        for t in range(32)
    ] + [
        pltpu.make_async_copy(left_h, left, in_sem.at[1]),
        pltpu.make_async_copy(right_h, right, in_sem.at[2]),
        pltpu.make_async_copy(accum_h, accum, in_sem.at[3]),
        pltpu.make_async_copy(master_h, master, in_sem.at[4]),
    ]
    row = f - lax.rem(f, 4)
    beside = [
        {"fsdp": row + lax.rem(f + 1, 4)},
        {"fsdp": row + lax.rem(f + 3, 4)},
        {"fsdp": lax.rem(f + 4, 16)},
        {"fsdp": lax.rem(f + 12, 16)},
    ]
    ring = [mate, {"rep": 2 * chip(1) + c}, {"rep": 2 * chip(-1) + c}, {"rep": 2 * chip(1) + 1 - c}]
    barrier = pltpu.get_barrier_semaphore()
    for peer in ring + beside:
        pl.semaphore_signal(barrier, 1, device_id=peer, device_id_type=MESH)

    def tell(turn):
        for peer in beside:
            pl.semaphore_signal(near_sem.at[turn], 1, device_id=peer, device_id_type=MESH)

    fetch_table = pltpu.make_async_copy(table_h, table, in_sem.at[5])
    fetch_table.start()
    for load in loads[:32]:
        load.start()
    fetch_table.wait()
    pltpu.make_async_copy(band, band, in_sem.at[0]).wait()
    for load in loads[32:]:
        load.start()

    def to_mate(j):
        return pltpu.make_async_remote_copy(
            src_ref=stage.at[j], dst_ref=sib.at[j], send_sem=sib_ssem, recv_sem=sib_rsem.at[j],
            device_id=mate, device_id_type=MESH,
        )

    def fill(j):
        hops, other = RS_ORDER[j]
        for k in range(2):
            stage[j, pl.ds(k * W, W), :] = band[table[4 * chip(-hops) + 2 * core(1 - other) + k]]

    for j in range(8):
        fill(j)
        if j == 0:
            pl.semaphore_wait(barrier, 8)
        to_mate(j).start()

    def pair(j, k, i, ident):
        own = band[ident, pl.ds(32 * i, 32), :].astype(f32)
        return own + sib[j, pl.ds(k * W + 32 * i, 32), :].astype(f32)

    def arrived(j, k, i):
        return recvq[j, k, pl.ds(32 * i, 32), :].astype(f32) * spread(recvs[j, k])

    def ahead(j):
        return {"rep": 2 * chip(1) + (core(RS_ORDER[j][1]) if RS_ORDER[j][0] == 1 else c)}

    def data_copy(j, k):
        return pltpu.make_async_remote_copy(
            src_ref=sendq.at[j, k], dst_ref=recvq.at[j, k], send_sem=q_ssem, recv_sem=q_rsem.at[j, k],
            device_id=ahead(j), device_id_type=MESH,
        )

    def scale_copy(j, k):
        return pltpu.make_async_remote_copy(
            src_ref=sends.at[j, k], dst_ref=recvs.at[j, k], send_sem=s_ssem.at[j, k], recv_sem=s_rsem.at[j, k],
            device_id=ahead(j), device_id_type=MESH,
        )

    def message(j, k):
        hops, other = RS_ORDER[j]
        ident = table[4 * chip(hops) + 2 * core(other) + k]
        if j >= 2:
            data_copy(j - 2, k).wait_recv()
            scale_copy(j - 2, k).wait_recv()
        most = jnp.full((8, 128), TINY, f32)
        for i in range(8):
            x = pair(j, k, i, ident)
            if j >= 2:
                x = x + arrived(j - 2, k, i)
            total[k, pl.ds(32 * i, 32), :] = x
            most = jnp.maximum(most, fold(jnp.abs(x), jnp.maximum))
        most = jnp.max(most, axis=0, keepdims=True)
        sends[j, k] = most * (1.0 / LEVELS)
        inverse = spread(LEVELS / most)
        for i in range(8):
            x = total[k, pl.ds(32 * i, 32), :] * inverse
            sendq[j, k, pl.ds(32 * i, 32), :] = jnp.round(x).astype(jnp.int32).astype(i16)
        data_copy(j, k).start()
        scale_copy(j, k).start()

    tell(0)
    for j in range(7):
        to_mate(j).wait_recv()
        for k in range(2):
            message(j, k)
        if j in (2, 4, 6):
            turn = j // 2 - 1
            pl.semaphore_wait(near_sem.at[turn], 4)
            if turn < 2:
                tell(turn + 1)
    to_mate(7).wait_recv()
    size = jnp.zeros((8, 128), f32)
    for k in range(2):
        ident = table[4 * z + 2 * c + k]
        for j in (5, 6):
            data_copy(j, k).wait_recv()
            scale_copy(j, k).wait_recv()
        for i in range(8):
            x = pair(7, k, i, ident) + arrived(5, k, i) + arrived(6, k, i)
            summed[k, pl.ds(32 * i, 32), :] = x
            size = size + fold(x * x, jnp.add)

    def norm_copy(stg, o):
        peer = {"rep": lax.rem(r + o, 16)} if stg == 0 else {"fsdp": lax.rem(f + o, 16)}
        return pltpu.make_async_remote_copy(
            src_ref=nsend.at[stg], dst_ref=nrecv.at[stg, o - 1], send_sem=n_ssem.at[stg], recv_sem=n_rsem.at[stg],
            device_id=peer, device_id_type=MESH,
        )

    def norm_all(stg):
        return pltpu.make_async_copy(nrecv.at[stg], nrecv.at[stg], n_rsem.at[stg])

    nsend[0] = size
    for o in range(1, 16):
        norm_copy(0, o).start()

    for load in loads[32:]:
        load.wait()

    def left_grams():
        for k in range(2):
            mats[2 * k] = gram_left(split(summed[k]))

    def right_grams():
        for k in range(2):
            mats[2 * k + 1] = gram_right(split(summed[k]))

    ident = eye()
    block(left_grams)
    norm_all(0).wait()
    for o in range(15):
        size = size + nrecv[0, o]
    nsend[1] = size
    for o in range(1, 16):
        norm_copy(1, o).start()
    def right_side():
        right_grams()
        for t in range(4):
            base = (left if t % 2 == 0 else right)[t // 2] + EPSILON * ident
            gram = mats[t]
            for part, term in enumerate((base * base, 2.0 * base * gram, gram * gram)):
                frob[t, part] = jnp.broadcast_to(jnp.sum(term, keepdims=True), (8, 128))

    block(right_side)
    norm_all(1).wait()
    for o in range(15):
        size = size + nrecv[1, o]
    norm_sq = jnp.sum(size, keepdims=True)
    clip = jnp.minimum(1.0, CLIP_NORM / (jnp.sqrt(norm_sq) + EPSILON))

    fourths, factors = [], []

    def near(cur):
        return (0.25 * cur).astype(bf16)

    def squared(n):
        return 1.5625 * ident - 2.5 * n.astype(f32) + dot(n, n)

    def advance_near(k, left_n, right_n):
        y = roots[k]
        high, low = split(y)
        y = 1.25 * y - (dot(left_n, high) + dot(left_n, low))
        high, low = split(y)
        roots[k] = 1.25 * y - (dot(high, right_n) + dot(low, right_n))

    def advance(k, left_factor, right_factor):
        roots[k] = mm(split(mm(left_factor, split(roots[k]))), right_factor)

    for k in range(2):
        for s in range(2):
            stats = left if s == 0 else right
            t = 2 * k + s
            clip2 = clip * clip
            a = stats[k] + clip2 * mats[t] + EPSILON * ident
            parts = [frob[t, part, 0:1, 0:1] for part in range(3)]
            zeta = 2.5 / jnp.sqrt(parts[0] + clip2 * (parts[1] + clip2 * parts[2]))
            cur = zeta * a
            fourths.append(jnp.sqrt(jnp.sqrt(zeta)))
            n = near(cur)
            factors.append(n)
            ss = split(squared(n))
            mats[t] = mm(split(mm(ss, split(cur))), ss)

    for k in range(2):
        roots[k] = (clip * fourths[2 * k] * fourths[2 * k + 1]) * summed[k]
        advance_near(k, factors[2 * k], factors[2 * k + 1])

    ada_sizes = []
    for k in range(2):
        g = clip * summed[k]
        ada = g / (jnp.sqrt(accum[k] + g * g) + EPSILON)
        ada_sizes.append(jnp.sqrt(jnp.sum(ada * ada, keepdims=True)))

    for sweep in range(ITERS - 2):
        curs = [mats[t] for t in range(4)]
        ns = [near(cur) for cur in curs]
        sss = [split(squared(n)) for n in ns]
        for k in range(2):
            advance_near(k, ns[2 * k], ns[2 * k + 1])
        uss = [split(mm(p, split(cur))) for p, cur in zip(sss, curs)]
        for t in range(4):
            mats[t] = mm(uss[t], sss[t])

    def last_factors(k):
        advance(k, *(split(1.25 * ident - 0.25 * mats[t]) for t in (2 * k, 2 * k + 1)))

    def finish(k):
        sham = roots[k]
        sham_size = jnp.sqrt(jnp.sum(sham * sham, keepdims=True))
        step = sham * (ada_sizes[k] / (sham_size + EPSILON))
        steps[k] = step
        ag[4 * z + 2 * c + k] = (master[k] - STEP_RATE * step).astype(bf16)

    def ag_copy(i, k, back=1):
        hops, other = AG_ORDER[i]
        slot = 4 * chip(back - hops) + 2 * core(other) + k
        return pltpu.make_async_remote_copy(
            src_ref=ag.at[slot], dst_ref=ag.at[slot], send_sem=ag_ssem, recv_sem=ag_rsem.at[i, k],
            device_id={"rep": 2 * chip(1) + c}, device_id_type=MESH,
        )

    def share(i, k):
        hops, other = AG_ORDER[i]
        slot = 4 * chip(-hops) + 2 * core(other) + k
        return pltpu.make_async_remote_copy(
            src_ref=ag.at[slot], dst_ref=ag.at[slot], send_sem=x_ssem, recv_sem=x_rsem,
            device_id=mate, device_id_type=MESH,
        )

    def own_share(k):
        slot = 4 * z + 2 * c + k
        return pltpu.make_async_remote_copy(
            src_ref=ag.at[slot], dst_ref=ag.at[slot], send_sem=x_ssem, recv_sem=own_rsem.at[k],
            device_id=mate, device_id_type=MESH,
        )

    def own_out(k):
        ag_copy(0, k).start()
        own_share(k).start()

    def mate_out(k):
        own_share(k).wait_recv()
        ag_copy(1, k).start()

    def drain(ref, sem):
        pltpu.make_async_copy(ref, ref, sem).wait()

    last_factors(0)
    finish(0)
    own_out(0)
    block(lambda: last_factors(1))
    mate_out(0)
    block(lambda: finish(1))
    own_out(1)
    mate_out(1)
    drain(stage, sib_ssem)
    drain(sendq, q_ssem)
    for j in range(7):
        for k in range(2):
            scale_copy(j, k).wait_send()
    for stg in range(2):
        drain(nrecv.at[stg], n_ssem.at[stg])
    for i in range(7):
        for k in range(2):
            ag_copy(i, k, 0).wait_recv()
            if i + 2 < 7:
                ag_copy(i + 2, k).start()
            share(i, k).start()

    drain(ag.at[pl.ds(0, 14)], ag_ssem)
    drain(ag.at[pl.ds(0, 16)], x_ssem)
    drain(ag.at[pl.ds(0, 14)], x_rsem)


def place(table, gath, steps_in, weights, steps, sems):
    for s in range(32):
        ident = table[s]
        top = pl.multiple_of((ident // 16) * W, W)
        lead = pl.multiple_of((ident % 16) * W, W)
        pltpu.make_async_copy(gath.at[s], weights.at[pl.ds(top, W), pl.ds(lead, W)], sems.at[0]).start()
    keep = pltpu.make_async_copy(steps_in, steps, sems.at[1])
    keep.start()
    pltpu.make_async_copy(gath, gath, sems.at[0]).wait()
    keep.wait()


def per_device(grad_parts, owner_table, left_stats, right_stats, accum, master):
    band = grad_parts[0]
    smem = pl.BlockSpec(memory_space=pltpu.SMEM)
    anyw = pl.BlockSpec(memory_space=pl.ANY)
    vmem = pl.BlockSpec(memory_space=pltpu.VMEM)
    tiles = (2, W, W)
    dma = pltpu.SemaphoreType.DMA
    steps, gath = pl.pallas_call(
        kernel,
        out_shape=(pltpu.VMEM(tiles, f32), pltpu.VMEM((32, W, W), bf16)),
        in_specs=[pl.BlockSpec(memory_space=pltpu.HBM)] * 6,
        out_specs=(vmem, vmem),
        scratch_shapes=[
            pltpu.SMEM((32,), jnp.int32),
            pltpu.VMEM((32, W, W), bf16),
            pltpu.VMEM(tiles, f32),
            pltpu.VMEM(tiles, f32),
            pltpu.VMEM(tiles, f32),
            pltpu.VMEM(tiles, f32),
            pltpu.VMEM((8, 2 * W, W), bf16),
            pltpu.VMEM((8, 2 * W, W), bf16),
            pltpu.VMEM(tiles, f32),
            pltpu.VMEM((7, 2, W, W), i16),
            pltpu.VMEM((7, 2, 1, 128), f32),
            pltpu.VMEM((7, 2, W, W), i16),
            pltpu.VMEM((7, 2, 1, 128), f32),
            pltpu.VMEM(tiles, f32),
            pltpu.VMEM((2, 8, 128), f32),
            pltpu.VMEM((2, 15, 8, 128), f32),
            pltpu.VMEM((4, W, W), f32),
            pltpu.VMEM(tiles, f32),
            pltpu.VMEM((4, 3, 8, 128), f32),
            dma((6,)), pltpu.SemaphoreType.REGULAR((3,)), dma, dma((8,)), dma, dma((7, 2)), dma((7, 2)), dma((7, 2)),
            dma((2,)), dma((2,)), dma, dma((7, 2)), dma, dma, dma((2,)),
        ],
        compiler_params=pltpu.CompilerParams(
            collective_id=0, has_side_effects=True, vmem_limit_bytes=58 << 20
        ),
        name="shampoo",
    )(owner_table, band, left_stats, right_stats, accum, master)
    weights, steps = pl.pallas_call(
        place,
        out_shape=(
            jax.ShapeDtypeStruct(band.shape, bf16),
            jax.ShapeDtypeStruct(tiles, f32),
        ),
        in_specs=[smem, vmem, vmem],
        out_specs=(anyw, anyw),
        scratch_shapes=[dma((2,))],
        compiler_params=pltpu.CompilerParams(vmem_limit_bytes=16 << 20),
        name="place",
    )(owner_table, gath, steps)
    return (steps, weights)


def solution(mesh):
    return jax.shard_map(
        per_device,
        mesh=mesh,
        in_specs=(
            P("rep", "fsdp", None),
            P(),
            P(("fsdp", "rep"), None, None),
            P(("fsdp", "rep"), None, None),
            P(("fsdp", "rep"), None, None),
            P(("fsdp", "rep"), None, None),
        ),
        out_specs=(P(("fsdp", "rep"), None, None), P("fsdp", None)),
        check_vma=False,
    )
```

```python
import functools
import jax
import jax.numpy as jnp
from jax import lax
from jax.experimental import pallas as pl
from jax.experimental.pallas import tpu as pltpu
from jax.sharding import PartitionSpec as P

ITERS = 8
EPSILON = 1e-06
STEP_RATE = 0.2
CLIP_NORM = 1.0
W = 256
LEVELS = 32767.0
TINY = 1e-30
f32, bf16, i16 = jnp.float32, jnp.bfloat16, jnp.int16
MESH = pl.DeviceIdType.MESH

RS_ORDER = ((4, 0), (3, 1), (3, 0), (2, 1), (2, 0), (1, 1), (1, 0), (0, 0))
AG_ORDER = ((1, 0), (1, 1), (2, 0), (2, 1), (3, 0), (3, 1), (4, 0))


def split(x):
    high = x.astype(bf16)
    return high, (x - high.astype(f32)).astype(bf16)


def dot(a, b):
    return jnp.dot(a, b, preferred_element_type=f32)


def mm(a, b):
    return dot(a[0], b[0]) + (dot(a[0], b[1]) + dot(a[1], b[0]))


def gram_left(a):
    def one(u, v):
        return lax.dot_general(u, v, (((1,), (1,)), ((), ())), preferred_element_type=f32)

    return one(a[0], a[0]) + (one(a[0], a[1]) + one(a[1], a[0]))


def gram_right(a):
    def one(u, v):
        return lax.dot_general(u, v, (((0,), (0,)), ((), ())), preferred_element_type=f32)

    return one(a[0], a[0]) + (one(a[0], a[1]) + one(a[1], a[0]))


def eye():
    rows = lax.broadcasted_iota(jnp.int32, (W, W), 0)
    return (rows == lax.broadcasted_iota(jnp.int32, (W, W), 1)).astype(f32)


def spread(scale):
    return jnp.broadcast_to(jnp.concatenate([scale, scale], axis=1), (32, W))


def fold(x, op):
    parts = [x[8 * i : 8 * i + 8, :] for i in range(4)]
    both = op(op(parts[0], parts[1]), op(parts[2], parts[3]))
    return op(both[:, :128], both[:, 128:])


def kernel(
    table_h, band_h, left_h, right_h, accum_h, master_h,
    steps, ag,
    table, band, left, right, accum, master,
    stage, sib, total, sendq, sends, recvq, recvs, summed, nsend, nrecv,
    mats, roots, frob,
    in_sem, near_sem, sib_ssem, sib_rsem, q_ssem, q_rsem, s_ssem, s_rsem,
    n_ssem, n_rsem, ag_ssem, ag_rsem, x_ssem, x_rsem, own_rsem,
):
    f = lax.axis_index("fsdp")
    r = lax.axis_index("rep")
    z = r // 2
    c = r - 2 * z
    mate = {"rep": r + 1 - 2 * c}
    once = jnp.minimum(r + 1, 1)

    def block(work):
        def body(i, carry):
            work()
            return carry

        lax.fori_loop(0, once, body, 0)

    chips = 8

    way = 2 * c - 1

    def chip(hops):
        return lax.rem(z + way * hops + chips, chips)

    def core(other):
        return 1 - c if other else c

    loads = [
        pltpu.make_async_copy(
            band_h.at[pl.ds(W * (t // 16), W), pl.ds(W * (t % 16), W)], band.at[t], in_sem.at[0]
        )
        for t in range(32)
    ] + [
        pltpu.make_async_copy(left_h, left, in_sem.at[1]),
        pltpu.make_async_copy(right_h, right, in_sem.at[2]),
        pltpu.make_async_copy(accum_h, accum, in_sem.at[3]),
        pltpu.make_async_copy(master_h, master, in_sem.at[4]),
    ]
    row = f - lax.rem(f, 4)
    beside = [
        {"fsdp": row + lax.rem(f + 1, 4)},
        {"fsdp": row + lax.rem(f + 3, 4)},
        {"fsdp": lax.rem(f + 4, 16)},
        {"fsdp": lax.rem(f + 12, 16)},
    ]
    ring = [mate, {"rep": 2 * chip(1) + c}, {"rep": 2 * chip(-1) + c}, {"rep": 2 * chip(1) + 1 - c}]
    barrier = pltpu.get_barrier_semaphore()
    for peer in ring + beside:
        pl.semaphore_signal(barrier, 1, device_id=peer, device_id_type=MESH)

    def tell(turn):
        for peer in beside:
            pl.semaphore_signal(near_sem.at[turn], 1, device_id=peer, device_id_type=MESH)

    fetch_table = pltpu.make_async_copy(table_h, table, in_sem.at[5])
    fetch_table.start()
    for load in loads[:32]:
        load.start()
    fetch_table.wait()
    pltpu.make_async_copy(band, band, in_sem.at[0]).wait()
    for load in loads[32:]:
        load.start()

    def to_mate(j, k):
        half = pl.ds(k * W, W)
        return pltpu.make_async_remote_copy(
            src_ref=stage.at[j, half], dst_ref=sib.at[j, half], send_sem=sib_ssem, recv_sem=sib_rsem.at[j, k],
            device_id=mate, device_id_type=MESH,
        )

    def fill(j, k):
        hops, other = RS_ORDER[j]
        stage[j, pl.ds(k * W, W), :] = band[table[4 * chip(-hops) + 2 * core(1 - other) + k]]

    for j in range(8):
        for k in range(2):
            fill(j, k)
            if j == 0 and k == 0:
                pl.semaphore_wait(barrier, 8)
            to_mate(j, k).start()

    def pair(j, k, i, ident):
        own = band[ident, pl.ds(32 * i, 32), :].astype(f32)
        return own + sib[j, pl.ds(k * W + 32 * i, 32), :].astype(f32)

    def arrived(j, k, i):
        return recvq[j, k, pl.ds(32 * i, 32), :].astype(f32) * spread(recvs[j, k])

    def ahead(j):
        return {"rep": 2 * chip(1) + (core(RS_ORDER[j][1]) if RS_ORDER[j][0] == 1 else c)}

    def data_copy(j, k):
        return pltpu.make_async_remote_copy(
            src_ref=sendq.at[j, k], dst_ref=recvq.at[j, k], send_sem=q_ssem, recv_sem=q_rsem.at[j, k],
            device_id=ahead(j), device_id_type=MESH,
        )

    def scale_copy(j, k):
        return pltpu.make_async_remote_copy(
            src_ref=sends.at[j, k], dst_ref=recvs.at[j, k], send_sem=s_ssem.at[j, k], recv_sem=s_rsem.at[j, k],
            device_id=ahead(j), device_id_type=MESH,
        )

    def message(j, k):
        hops, other = RS_ORDER[j]
        ident = table[4 * chip(hops) + 2 * core(other) + k]
        if j >= 2:
            data_copy(j - 2, k).wait_recv()
            scale_copy(j - 2, k).wait_recv()
        most = jnp.full((8, 128), TINY, f32)
        for i in range(8):
            x = pair(j, k, i, ident)
            if j >= 2:
                x = x + arrived(j - 2, k, i)
            total[k, pl.ds(32 * i, 32), :] = x
            most = jnp.maximum(most, fold(jnp.abs(x), jnp.maximum))
        most = jnp.max(most, axis=0, keepdims=True)
        sends[j, k] = most * (1.0 / LEVELS)
        inverse = spread(LEVELS / most)
        for i in range(8):
            x = total[k, pl.ds(32 * i, 32), :] * inverse
            sendq[j, k, pl.ds(32 * i, 32), :] = jnp.round(x).astype(jnp.int32).astype(i16)
        data_copy(j, k).start()
        scale_copy(j, k).start()

    tell(0)
    for j in range(7):
        for k in range(2):
            to_mate(j, k).wait_recv()
            message(j, k)
        if j in (2, 4, 6):
            turn = j // 2 - 1
            pl.semaphore_wait(near_sem.at[turn], 4)
            if turn < 2:
                tell(turn + 1)
    for k in range(2):
        to_mate(7, k).wait_recv()
    size = jnp.zeros((8, 128), f32)
    for k in range(2):
        ident = table[4 * z + 2 * c + k]
        for j in (5, 6):
            data_copy(j, k).wait_recv()
            scale_copy(j, k).wait_recv()
        for i in range(8):
            x = pair(7, k, i, ident) + arrived(5, k, i) + arrived(6, k, i)
            summed[k, pl.ds(32 * i, 32), :] = x
            size = size + fold(x * x, jnp.add)

    def norm_copy(stg, o):
        peer = {"rep": lax.rem(r + o, 16)} if stg == 0 else {"fsdp": lax.rem(f + o, 16)}
        return pltpu.make_async_remote_copy(
            src_ref=nsend.at[stg], dst_ref=nrecv.at[stg, o - 1], send_sem=n_ssem.at[stg], recv_sem=n_rsem.at[stg],
            device_id=peer, device_id_type=MESH,
        )

    def norm_all(stg):
        return pltpu.make_async_copy(nrecv.at[stg], nrecv.at[stg], n_rsem.at[stg])

    nsend[0] = size
    for o in range(1, 16):
        norm_copy(0, o).start()

    for load in loads[32:]:
        load.wait()

    def left_grams():
        for k in range(2):
            mats[2 * k] = gram_left(split(summed[k]))

    def right_grams():
        for k in range(2):
            mats[2 * k + 1] = gram_right(split(summed[k]))

    ident = eye()
    block(left_grams)
    norm_all(0).wait()
    for o in range(15):
        size = size + nrecv[0, o]
    nsend[1] = size
    for o in range(1, 16):
        norm_copy(1, o).start()
    def right_side():
        right_grams()
        for t in range(4):
            base = (left if t % 2 == 0 else right)[t // 2] + EPSILON * ident
            gram = mats[t]
            for part, term in enumerate((base * base, 2.0 * base * gram, gram * gram)):
                frob[t, part] = jnp.broadcast_to(jnp.sum(term, keepdims=True), (8, 128))

    block(right_side)
    norm_all(1).wait()
    for o in range(15):
        size = size + nrecv[1, o]
    norm_sq = jnp.sum(size, keepdims=True)
    clip = jnp.minimum(1.0, CLIP_NORM / (jnp.sqrt(norm_sq) + EPSILON))

    fourths, factors = [], []

    def near(cur):
        return (0.25 * cur).astype(bf16)

    def squared(n):
        return 1.5625 * ident - 2.5 * n.astype(f32) + dot(n, n)

    def advance_near(k, left_n, right_n):
        y = roots[k]
        high, low = split(y)
        y = 1.25 * y - (dot(left_n, high) + dot(left_n, low))
        high, low = split(y)
        roots[k] = 1.25 * y - (dot(high, right_n) + dot(low, right_n))

    def advance(k, left_factor, right_factor):
        roots[k] = mm(split(mm(left_factor, split(roots[k]))), right_factor)

    for k in range(2):
        for s in range(2):
            stats = left if s == 0 else right
            t = 2 * k + s
            clip2 = clip * clip
            a = stats[k] + clip2 * mats[t] + EPSILON * ident
            parts = [frob[t, part, 0:1, 0:1] for part in range(3)]
            zeta = 2.5 / jnp.sqrt(parts[0] + clip2 * (parts[1] + clip2 * parts[2]))
            cur = zeta * a
            fourths.append(jnp.sqrt(jnp.sqrt(zeta)))
            n = near(cur)
            factors.append(n)
            ss = split(squared(n))
            mats[t] = mm(split(mm(ss, split(cur))), ss)

    for k in range(2):
        roots[k] = (clip * fourths[2 * k] * fourths[2 * k + 1]) * summed[k]
        advance_near(k, factors[2 * k], factors[2 * k + 1])

    ada_sizes = []
    for k in range(2):
        g = clip * summed[k]
        ada = g / (jnp.sqrt(accum[k] + g * g) + EPSILON)
        ada_sizes.append(jnp.sqrt(jnp.sum(ada * ada, keepdims=True)))

    def sweep(group):
        ts = [t for k in group for t in (2 * k, 2 * k + 1)]
        curs = {t: mats[t] for t in ts}
        ns = {t: near(curs[t]) for t in ts}
        sss = {t: split(squared(ns[t])) for t in ts}
        for k in group:
            advance_near(k, ns[2 * k], ns[2 * k + 1])
        uss = {t: split(mm(sss[t], split(curs[t]))) for t in ts}
        for t in ts:
            mats[t] = mm(uss[t], sss[t])

    for _ in range(ITERS - 4):
        sweep((0, 1))
    for _ in range(2):
        sweep((0,))

    def last_factors(k):
        advance(k, *(split(1.25 * ident - 0.25 * mats[t]) for t in (2 * k, 2 * k + 1)))

    def finish(k):
        sham = roots[k]
        sham_size = jnp.sqrt(jnp.sum(sham * sham, keepdims=True))
        step = sham * (ada_sizes[k] / (sham_size + EPSILON))
        steps[k] = step
        ag[4 * z + 2 * c + k] = (master[k] - STEP_RATE * step).astype(bf16)

    def ag_copy(i, k, back=1):
        hops, other = AG_ORDER[i]
        slot = 4 * chip(back - hops) + 2 * core(other) + k
        return pltpu.make_async_remote_copy(
            src_ref=ag.at[slot], dst_ref=ag.at[slot], send_sem=ag_ssem, recv_sem=ag_rsem.at[i, k],
            device_id={"rep": 2 * chip(1) + c}, device_id_type=MESH,
        )

    def share(i, k):
        hops, other = AG_ORDER[i]
        slot = 4 * chip(-hops) + 2 * core(other) + k
        return pltpu.make_async_remote_copy(
            src_ref=ag.at[slot], dst_ref=ag.at[slot], send_sem=x_ssem, recv_sem=x_rsem,
            device_id=mate, device_id_type=MESH,
        )

    def own_share(k):
        slot = 4 * z + 2 * c + k
        return pltpu.make_async_remote_copy(
            src_ref=ag.at[slot], dst_ref=ag.at[slot], send_sem=x_ssem, recv_sem=own_rsem.at[k],
            device_id=mate, device_id_type=MESH,
        )

    def own_out(k):
        ag_copy(0, k).start()
        own_share(k).start()

    def mate_out(k):
        own_share(k).wait_recv()
        ag_copy(1, k).start()

    def drain(ref, sem):
        pltpu.make_async_copy(ref, ref, sem).wait()

    last_factors(0)
    finish(0)
    own_out(0)

    block(lambda: sweep((1,)))
    mate_out(0)

    def second():
        sweep((1,))
        last_factors(1)

    block(second)
    block(lambda: finish(1))
    own_out(1)
    mate_out(1)
    drain(stage, sib_ssem)
    drain(sendq, q_ssem)
    for j in range(7):
        for k in range(2):
            scale_copy(j, k).wait_send()
    for stg in range(2):
        drain(nrecv.at[stg], n_ssem.at[stg])
    for i in range(7):
        for k in range(2):
            ag_copy(i, k, 0).wait_recv()
            if i + 2 < 7:
                ag_copy(i + 2, k).start()
            share(i, k).start()

    drain(ag.at[pl.ds(0, 14)], ag_ssem)
    drain(ag.at[pl.ds(0, 16)], x_ssem)
    drain(ag.at[pl.ds(0, 14)], x_rsem)


def place(table, gath, steps_in, weights, steps, sems):
    for s in range(32):
        ident = table[s]
        top = pl.multiple_of((ident // 16) * W, W)
        lead = pl.multiple_of((ident % 16) * W, W)
        pltpu.make_async_copy(gath.at[s], weights.at[pl.ds(top, W), pl.ds(lead, W)], sems.at[0]).start()
    keep = pltpu.make_async_copy(steps_in, steps, sems.at[1])
    keep.start()
    pltpu.make_async_copy(gath, gath, sems.at[0]).wait()
    keep.wait()


def per_device(grad_parts, owner_table, left_stats, right_stats, accum, master):
    band = grad_parts[0]
    smem = pl.BlockSpec(memory_space=pltpu.SMEM)
    anyw = pl.BlockSpec(memory_space=pl.ANY)
    vmem = pl.BlockSpec(memory_space=pltpu.VMEM)
    tiles = (2, W, W)
    dma = pltpu.SemaphoreType.DMA
    steps, gath = pl.pallas_call(
        kernel,
        out_shape=(pltpu.VMEM(tiles, f32), pltpu.VMEM((32, W, W), bf16)),
        in_specs=[pl.BlockSpec(memory_space=pltpu.HBM)] * 6,
        out_specs=(vmem, vmem),
        scratch_shapes=[
            pltpu.SMEM((32,), jnp.int32),
            pltpu.VMEM((32, W, W), bf16),
            pltpu.VMEM(tiles, f32),
            pltpu.VMEM(tiles, f32),
            pltpu.VMEM(tiles, f32),
            pltpu.VMEM(tiles, f32),
            pltpu.VMEM((8, 2 * W, W), bf16),
            pltpu.VMEM((8, 2 * W, W), bf16),
            pltpu.VMEM(tiles, f32),
            pltpu.VMEM((7, 2, W, W), i16),
            pltpu.VMEM((7, 2, 1, 128), f32),
            pltpu.VMEM((7, 2, W, W), i16),
            pltpu.VMEM((7, 2, 1, 128), f32),
            pltpu.VMEM(tiles, f32),
            pltpu.VMEM((2, 8, 128), f32),
            pltpu.VMEM((2, 15, 8, 128), f32),
            pltpu.VMEM((4, W, W), f32),
            pltpu.VMEM(tiles, f32),
            pltpu.VMEM((4, 3, 8, 128), f32),
            dma((6,)), pltpu.SemaphoreType.REGULAR((3,)), dma, dma((8, 2)), dma, dma((7, 2)), dma((7, 2)), dma((7, 2)),
            dma((2,)), dma((2,)), dma, dma((7, 2)), dma, dma, dma((2,)),
        ],
        compiler_params=pltpu.CompilerParams(
            collective_id=0, has_side_effects=True, vmem_limit_bytes=58 << 20
        ),
        name="shampoo",
    )(owner_table, band, left_stats, right_stats, accum, master)
    weights, steps = pl.pallas_call(
        place,
        out_shape=(
            jax.ShapeDtypeStruct(band.shape, bf16),
            jax.ShapeDtypeStruct(tiles, f32),
        ),
        in_specs=[smem, vmem, vmem],
        out_specs=(anyw, anyw),
        scratch_shapes=[dma((2,))],
        compiler_params=pltpu.CompilerParams(vmem_limit_bytes=16 << 20),
        name="place",
    )(owner_table, gath, steps)
    return (steps, weights)


def solution(mesh):
    return jax.shard_map(
        per_device,
        mesh=mesh,
        in_specs=(
            P("rep", "fsdp", None),
            P(),
            P(("fsdp", "rep"), None, None),
            P(("fsdp", "rep"), None, None),
            P(("fsdp", "rep"), None, None),
            P(("fsdp", "rep"), None, None),
        ),
        out_specs=(P(("fsdp", "rep"), None, None), P("fsdp", None)),
        check_vma=False,
    )
```
